256 devices in a mesh: member: 8 (over y_hi, x), dp: 32 (over z, y_lo, core).
Axes of the slice: x: 4, y: 4 (y_hi: 2, y_lo: 2; y = y_hi * 2 + y_lo), z: 8, core: 2. Of those that a mesh axis runs over, the one named last changes fastest.
Arguments:
- inputs: bfloat16 [8, 4096, 896], P('member', 'dp'), may hold values from -6 to 6
- cotangent: bfloat16 [8, 4096, 896], P('member', 'dp'), may hold values from -6 to 6
- counts: int32 [8, 4096], P('member', 'dp'), may hold values from 0 to 3
- pre_hidden: bfloat16 [8, 15360, 4096], P('member', 'dp'), may hold values from -6 to 6
- pre_out: bfloat16 [8, 4096, 896], P('member', 'dp'), may hold values from -6 to 6
- w_in: bfloat16 [15360, 896], P('dp'), may hold values from -0.1875 to 0.1875
- w_out: bfloat16 [15360, 896], P('dp'), may hold values from -0.046875 to 0.046875
- r_in: float32 [8, 896], P('member'), may hold values from 0.1 to 1.9
- s_in: float32 [8, 15360], P('member', 'dp'), may hold values from 0.1 to 1.9
- r_out: float32 [8, 15360], P('member', 'dp'), may hold values from 0.1 to 1.9
- s_out: float32 [8, 896], P('member'), may hold values from 0.1 to 1.9
Outputs:
- grad_inputs: float32 [8, 4096, 896], P('member', 'dp')
- grad_w_in: float32 [15360, 896], P('dp')
- grad_w_out: float32 [15360, 896], P('dp')
- grad_r_in: float32 [8, 896], P('member')
- grad_s_in: float32 [8, 15360], P('member', 'dp')
- grad_r_out: float32 [8, 15360], P('member', 'dp')
- grad_s_out: float32 [8, 896], P('member')
The draws below stay inside these ranges and needn't reach their ends.
All inputs are finite; a program needn't handle non-finite values.
Results may differ from the reference program's by a relative error of at most 0.005.
Values may be sent and summed in bfloat16 or wider, within the bound.
A program may use at most 128 MiB of HBM per device.

```python
import jax
import jax.numpy as jnp
from jax import lax

D = 896
FF = 15360
MEMBERS = 8
TOKENS = 4096


def plant(values, rng, smallest, top_value):
    spot = [jax.random.randint(jax.random.fold_in(rng, axis), (), 0, length) for axis, length in enumerate(values.shape)]
    longest = values.shape.index(max(values.shape))
    next_to = spot[:longest] + [(spot[longest] + 1) % values.shape[longest]] + spot[longest + 1:]
    return values.at[tuple(spot)].set(smallest).at[tuple(next_to)].set(top_value)


def shard_levels(stream_key, shape, split, least, top_value):
    def one(dim, shards_of):
        heights = jax.random.uniform(jax.random.fold_in(jax.random.fold_in(stream_key, 6), dim), (shards_of,), jnp.float32, least / len(split), top_value / len(split))
        return jnp.repeat(jnp.exp(heights), shape[dim] // shards_of).reshape((-1,) + (1,) * (len(shape) - dim - 1))

    loudness = one(*split[0])
    for cut in split[1:]:
        loudness = loudness * one(*cut)
    return loudness


def scatter_about(rng, extent, scale, reach, pieces=(), dtype=jnp.bfloat16):
    result = jax.random.normal(rng, extent, jnp.float32) * scale
    if len(pieces) > 0:
        result = shard_levels(rng, extent, pieces, -0.22, 0.18) * result
    return jnp.clip(result, min=-reach, max=reach).astype(dtype)


def setup_inputs(seed: int = 0) -> dict:
    streams_of = jax.random.split(jax.random.key(seed), 12)
    inputs = scatter_about(streams_of[0], (MEMBERS, TOKENS, D), 1.0, 6.0, ((0, 8), (1, 32)))
    cotangent = scatter_about(streams_of[1], (MEMBERS, TOKENS, D), 1.0, 6.0, ((0, 8), (1, 32)))
    counts = plant(jax.random.randint(streams_of[2], (MEMBERS, TOKENS), 0, 4), jax.random.fold_in(streams_of[2], 1), 0, 3).astype(jnp.int32)
    pre_hidden = scatter_about(streams_of[3], (MEMBERS, FF, TOKENS), 1.0, 6.0, ((0, 8), (1, 32)))
    pre_out = scatter_about(streams_of[4], (MEMBERS, TOKENS, D), 1.0, 6.0, ((0, 8), (1, 32)))
    w_in = scatter_about(streams_of[5], (FF, D), D ** -0.5, 0.1875, ((0, 32),))
    w_out = scatter_about(streams_of[6], (FF, D), FF ** -0.5, 0.046875, ((0, 32),))
    r_in = jnp.clip(1.0 + 0.18 * jax.random.normal(streams_of[7], (MEMBERS, D), jnp.float32), 0.1, 1.9)
    s_in = jnp.clip(1.0 + 0.18 * jax.random.normal(streams_of[8], (MEMBERS, FF), jnp.float32), 0.1, 1.9)
    r_out = jnp.clip(1.0 + 0.18 * jax.random.normal(streams_of[9], (MEMBERS, FF), jnp.float32), 0.1, 1.9)
    s_out = jnp.clip(1.0 + 0.18 * jax.random.normal(streams_of[10], (MEMBERS, D), jnp.float32), 0.1, 1.9)
    return dict(inputs=inputs, cotangent=cotangent, counts=counts, pre_hidden=pre_hidden, pre_out=pre_out, w_in=w_in, w_out=w_out, r_in=r_in, s_in=s_in, r_out=r_out, s_out=s_out)


def gelu_pair(value):
    normal_cdf = 0.5 * (1.0 + jax.scipy.special.erf(value * 0.7071067811865476))
    slope = normal_cdf + value * jnp.exp(-0.5 * value * value) * 0.3989422804014327
    return (value * normal_cdf, slope)

def reference(inputs, cotangent, counts, pre_hidden, pre_out, w_in, w_out, r_in, s_in, r_out, s_out):
    token_scale = 1.0 / jnp.sqrt(jnp.float32(TOKENS))
    weight_scale = 1.0 / jnp.sqrt(jnp.float32(MEMBERS * TOKENS))

    def member_step(carry, items):
        acc_in, acc_out = carry
        x_m, dy_m, cnt_m, pre_m, z_m, r1, s1, r2, s2 = items
        weighted = dy_m.astype(jnp.float32) * cnt_m.astype(jnp.float32)[:, None]
        g_s_out = lax.optimization_barrier(jnp.sum(weighted * z_m.astype(jnp.float32), axis=0)) * token_scale
        grad_z = (weighted * s2[None, :]).astype(jnp.bfloat16)
        scaled_in = (x_m.astype(jnp.float32) * r1[None, :]).astype(jnp.bfloat16)
        pre_f = pre_m.astype(jnp.float32)
        act = pre_f * s1[:, None]
        gelu_val, slope = gelu_pair(act)
        hidden = (gelu_val * r2[:, None]).astype(jnp.bfloat16)
        grad_u = lax.dot_general(w_out, grad_z, (((1,), (1,)), ((), ())), preferred_element_type=jnp.float32)
        acc_out = acc_out + jnp.dot(hidden, grad_z, preferred_element_type=jnp.float32)
        g_r_out = lax.optimization_barrier(jnp.sum(grad_u * gelu_val, axis=1)) * token_scale
        grad_act = grad_u * r2[:, None] * slope
        g_s_in = lax.optimization_barrier(jnp.sum(grad_act * pre_f, axis=1)) * token_scale
        grad_pre = (grad_act * s1[:, None]).astype(jnp.bfloat16)
        acc_in = acc_in + jnp.dot(grad_pre, scaled_in, preferred_element_type=jnp.float32)
        grad_h = lax.dot_general(grad_pre, w_in, (((0,), (0,)), ((), ())), preferred_element_type=jnp.float32)
        g_x = grad_h * r1[None, :]
        g_r_in = lax.optimization_barrier(jnp.sum(grad_h * x_m.astype(jnp.float32), axis=0)) * token_scale
        return ((acc_in, acc_out), (g_x, g_r_in, g_s_in, g_r_out, g_s_out))
    start = (jnp.zeros((FF, D), jnp.float32), jnp.zeros((FF, D), jnp.float32))
    (acc_in, acc_out), outs = lax.scan(member_step, start, (inputs, cotangent, counts, pre_hidden, pre_out, r_in, s_in, r_out, s_out))
    g_x, g_r_in, g_s_in, g_r_out, g_s_out = outs
    return (g_x, acc_in * weight_scale, acc_out * weight_scale, g_r_in, g_s_in, g_r_out, g_s_out)
```

```python
import functools

import jax
import jax.numpy as jnp
from jax import lax
from jax.experimental import pallas as pl
from jax.experimental.pallas import tpu as pltpu
from jax.sharding import PartitionSpec as P

MESH = pl.DeviceIdType.MESH
BF = jnp.bfloat16
F32 = jnp.float32

NZ = 8
TB = 128
D = 896
FB = 480
NF = 2 * FB
NH = 2

HOPS = (
    (0, (0, 0), (7, 0)), (1, (0, 0), (1, 0)), (2, (0, 0), (0, 1)),
    (0, (7, 0), (6, 0)), (1, (1, 0), (2, 0)), (2, (7, 0), (7, 1)),
    (0, (6, 0), (5, 0)), (1, (2, 0), (3, 0)), (2, (1, 0), (1, 1)),
    (0, (5, 0), (4, 0)), (1, (1, 1), (2, 1)), (2, (6, 0), (6, 1)),
    (0, (6, 1), (5, 1)), (1, (2, 1), (3, 1)), (2, (4, 0), (4, 1)),
)
ORDER = (0, 7, 1, 2, 6, 5, 3, 4)


def kernel(
    x_ref, dy_ref, cnt_ref, ph_ref, po_ref, wi_ref, wo_ref, ri_ref, si_ref, ro_ref, so_ref,
    gx_ref, gwi_ref, gwo_ref, gri_ref, gsi_ref, gro_ref, gso_ref,
    pre, slope, hid, gp, z_all, in_all, wo, wi, wt, rbuf, sbuf, acc_ro, acc_si, acc_in,
    col_s, col_r, part, sib_out, sib_in, mem_out, mem_x, mem_h, mem_all, vec_out, vec_in, vec_z,
    ring_s, ring_r, pre_l, pre_s, pre_r, w_l, w_s, w_r, col_ss, col_sr, acc_ss, acc_sr,
    sib_ss, sib_sr, x_s, x_r, h_s, h_r, all_s, all_r, vec_ss, vec_sr, vz_s, vz_r,
):
    m, d = lax.axis_index("member"), lax.axis_index("dp")
    z, y, c = d // 4, (d // 2) % 2, d % 2
    yh, x = m // 4, m % 4
    zp = (m, lax.rem(z + 1, NZ) * 4 + y * 2 + c)
    zm = (m, lax.rem(z + NZ - 1, NZ) * 4 + y * 2 + c)
    yo = (m, z * 4 + (1 - y) * 2 + c)
    co = (m, z * 4 + y * 2 + (1 - c))
    xs = [(yh * 4 + lax.rem(x + k, 4), d) for k in (1, 2, 3)]
    ho = ((1 - yh) * 4 + x, d)
    sent = []

    def send(src, dst, ss, rs, dev):
        copy = pltpu.make_async_remote_copy(
            src_ref=src, dst_ref=dst, send_sem=ss, recv_sem=rs, device_id=dev, device_id_type=MESH
        )
        copy.start()
        sent.append(copy)
        return copy

    barrier = pltpu.get_barrier_semaphore()
    for dev in (zp, zm, yo, co, ho, *xs):
        pl.semaphore_signal(barrier, inc=1, device_id=dev, device_id_type=MESH)

    local = []
    for i, s in enumerate(ORDER):
        zs = lax.rem(z + s, NZ)
        for r in range(2):
            yy = y if r == 0 else 1 - y
            col = pl.multiple_of((zs * 4 + yy * 2 + c) * TB, TB)
            copy = pltpu.make_async_copy(
                ph_ref.at[:, pl.ds(col, TB)], pre.at[s, pl.ds(0, FB), pl.ds(r * TB, TB)], pre_l.at[s, r]
            )
            copy.start()
            local.append(copy)
    w_copies = []
    for i, (src, dst) in enumerate(((wo_ref, wo), (wi_ref, wi))):
        copy = pltpu.make_async_copy(src, dst.at[pl.ds(0, FB)], w_l.at[i])
        copy.start()
        w_copies.append(copy)

    cnt = jnp.broadcast_to(cnt_ref[...].astype(F32), (TB, TB)).T
    for j in range(D // 128):
        cs = pl.ds(j * 128, 128)
        weighted = dy_ref[:, cs].astype(F32) * cnt
        z_all[0, pl.ds(0, TB), cs] = (weighted * so_ref[:, cs]).astype(BF)
        in_all[0, pl.ds(0, TB), cs] = (x_ref[:, cs].astype(F32) * ri_ref[:, cs]).astype(BF)
        vec_out[0, pl.ds(0, 1), cs] = jnp.sum(weighted * po_ref[:, cs].astype(F32), axis=0, keepdims=True)

    pl.semaphore_wait(barrier, 8)

    TP = TB // NH

    def gather_send(u, buf, step, h):
        for k in range(3 * step, 3 * step + 3):
            way, (ss, sr), (ds, dr) = HOPS[k]
            send(
                buf.at[ss, pl.ds(sr * TB + h * TP, TP)], buf.at[ds, pl.ds(dr * TB + h * TP, TP)],
                ring_s.at[u, k, h], ring_r.at[u, k, h], (zp, zm, yo)[way],
            )

    def gather_wait(u, buf, step, h):
        for k in range(3 * step, 3 * step + 3):
            way, _, (ds, dr) = HOPS[k]
            part_ref = buf.at[ds, pl.ds(dr * TB + h * TP, TP)]
            pltpu.make_async_remote_copy(
                src_ref=part_ref, dst_ref=part_ref, send_sem=ring_s.at[u, k, h], recv_sem=ring_r.at[u, k, h],
                device_id=(zp, zm, yo)[way], device_id_type=MESH,
            ).wait_recv()

    for h in range(NH):
        gather_send(0, z_all, 0, h)

    pre_in = {}
    for s in ORDER:
        zs = lax.rem(z + s, NZ)
        for r in range(2):
            yy = y if r == 0 else 1 - y
            col = pl.multiple_of((zs * 4 + yy * 2 + (1 - c)) * TB, TB)
            pre_in[s, r] = send(
                ph_ref.at[:, pl.ds(col, TB)], pre.at[s, pl.ds(FB, FB), pl.ds(r * TB, TB)],
                pre_s.at[s, r], pre_r.at[s, r], co,
            )
        if s == 0:
            col_s[pl.ds(0, FB)] = jnp.broadcast_to(si_ref[...], (128, FB)).T
            col_r[pl.ds(0, FB)] = jnp.broadcast_to(ro_ref[...], (128, FB)).T
            col_in = [
                send(b.at[pl.ds(0, FB)], b.at[pl.ds(FB, FB)], col_ss.at[i], col_sr.at[i], co)
                for i, b in enumerate((col_s, col_r))
            ]
        if s == 7:
            w_in = [
                send(src, dst.at[pl.ds(FB, FB)], w_s.at[i], w_r.at[i], co)
                for i, (src, dst) in enumerate(((wo_ref, wo), (wi_ref, wi)))
            ]
    vec_out[0, pl.ds(2, 6)] = jnp.zeros((6, D), F32)
    acc_ro[...] = jnp.zeros_like(acc_ro)
    acc_si[...] = jnp.zeros_like(acc_si)

    GT = 32

    def gelu(s, side):
        if side == 0:
            for r in range(2):
                local[2 * ORDER.index(s) + r].wait()
        else:
            for r in range(2):
                pre_in[s, r].wait_recv()

        def tile(i, _):
            rows = pl.ds(pl.multiple_of(side * FB + i * GT, GT), GT)
            sc, rc = col_s[rows], col_r[rows]
            for j in range(2):
                cs = pl.ds(j * 128, 128)
                v = pre[s, rows, cs].astype(F32) * sc
                cdf = 0.5 * (1.0 + lax.erf(v * 0.7071067811865476))
                hid[s, rows, cs] = (v * cdf * rc).astype(BF)
                pdf = jnp.exp(-0.5 * v * v) * 0.3989422804014327
                slope[s, rows, cs] = (cdf + v * pdf) * rc
            return 0

        lax.fori_loop(0, FB // GT, tile, 0)

    UT = 240

    def grad_pre(s):
        def tile(i, _):
            rows = pl.ds(pl.multiple_of(i * UT, 16), UT)
            u = lax.dot_general(wo[rows], z_all[s], (((1,), (1,)), ((), ())), preferred_element_type=F32)
            sc = col_s[rows]
            q = u * hid[s, rows].astype(F32)
            acc_ro[rows] += q[:, :128] + q[:, 128:]
            a = u * slope[s, rows]
            q = a * pre[s, rows].astype(F32)
            acc_si[rows] += q[:, :128] + q[:, 128:]
            gp[s, rows, pl.ds(0, 128)] = (a[:, :128] * sc).astype(BF)
            gp[s, rows, pl.ds(128, 128)] = (a[:, 128:] * sc).astype(BF)
            return 0

        lax.fori_loop(0, NF // UT, tile, 0)

    HT = 448

    def grad_h(s):
        def tile(i, _):
            rows = pl.ds(pl.multiple_of(i * HT, 16), HT)
            slope[s, rows] = jnp.dot(wt[rows], gp[s], preferred_element_type=F32)
            return 0

        lax.fori_loop(0, D // HT, tile, 0)

    WT = 240

    def grad_w(out, lhs, rhs, side, slots, first):
        def tile(i, _):
            rows = pl.ds(pl.multiple_of(i * WT, 16), WT)
            src = pl.ds(pl.multiple_of(side * FB + i * WT, 16), WT)
            for n, s in enumerate(slots):
                t = jnp.dot(lhs[s, src], rhs[s], preferred_element_type=F32)
                if first and n == 0:
                    out[rows] = t
                else:
                    out[rows] += t
            return 0

        lax.fori_loop(0, FB // WT, tile, 0)

    outs = (gwo_ref, gwi_ref)
    stage = {}

    def piece(xx):
        return pl.ds(pl.multiple_of(112 * xx + 16 * (xx // 2), 16), 128)

    def w_sib(g):
        sib_out[g] = part[...].astype(BF)
        stage["sib", g] = send(sib_out.at[g], sib_in.at[g], sib_ss.at[g], sib_sr.at[g], co)

    def w_x(g):
        stage["sib", g].wait_recv()
        outs[g][...] += sib_in[g].astype(F32)
        mem_out[g] = outs[g][...].astype(BF)
        stage["x", g] = [
            send(mem_out.at[g, piece(lax.rem(x + k, 4))], mem_x.at[g, k - 1], x_s.at[g, k - 1], x_r.at[g, k - 1], xs[k - 1])
            for k in (1, 2, 3)
        ]

    def w_h(g):
        for copy in stage["x", g]:
            copy.wait_recv()
        total = outs[g][piece(x)]
        for k in range(3):
            total += mem_x[g, k].astype(F32)
        mem_h[g, 0] = total.astype(BF)
        stage["h", g] = send(mem_h.at[g, 0], mem_h.at[g, 1], h_s.at[g], h_r.at[g], ho)

    def w_all(g):
        stage["h", g].wait_recv()
        mem_all[g, 0] = (mem_h[g, 0].astype(F32) + mem_h[g, 1].astype(F32)).astype(BF)
        stage["all", g] = [
            send(mem_all.at[g, 0], mem_all.at[g, k], all_s.at[g, k - 1], all_r.at[g, k - 1], xs[k - 1])
            for k in (1, 2, 3)
        ]

    def w_end(g):
        for copy in stage["all", g]:
            copy.wait_recv()
        for xx in range(4):
            rows = pl.ds(112 * xx + 16 * (xx // 2), 128)
            outs[g][rows] = mem_all[g, lax.rem(x + 4 - xx, 4)].astype(F32) * (32768.0**-0.5)

    def v_part(side, grads):
        t = jnp.sum(wi[pl.ds(side * FB, FB)].astype(F32) * grads[...], axis=0, keepdims=True)
        if side == 1:
            vec_out[0, pl.ds(1, 1)] = t
        else:
            vec_out[0, pl.ds(1, 1)] += t

    def v_pair(i, dev):
        stage["v", i] = send(vec_out.at[i], vec_in.at[i], vec_ss.at[i], vec_sr.at[i], dev)

    def v_sum(i):
        stage["v", i].wait_recv()
        t = vec_out[i] + vec_in[i]
        if i == 0:
            vec_out[1] = t
        else:
            vec_z[0] = t

    def v_send(k):
        stage["va", k] = send(vec_z.at[(8 - k) % 8], vec_z.at[7 - k], vz_s.at[0, k], vz_r.at[0, k], zp)
        if k < 3:
            stage["vb", k] = send(vec_z.at[k], vec_z.at[k + 1], vz_s.at[1, k], vz_r.at[1, k], zm)

    def v_wait(k):
        stage["va", k].wait_recv()
        if k < 3:
            stage["vb", k].wait_recv()

    def v_end():
        total = vec_z[lax.rem(NZ - z, NZ)]
        for s in range(1, NZ):
            total += vec_z[lax.rem(s + NZ - z, NZ)]
        gso_ref[...] = total[0:1] * (1.0 / 64.0)
        gri_ref[...] = total[1:2] / ri_ref[...] * (1.0 / 64.0)

    def acc_send():
        stage["acc"] = [
            send(b.at[pl.ds(FB, FB)], acc_in.at[i], acc_ss.at[i], acc_sr.at[i], co)
            for i, b in enumerate((acc_ro, acc_si))
        ]

    def acc_end():
        for copy in stage["acc"]:
            copy.wait_recv()
        t = (acc_ro[pl.ds(0, FB)] + acc_in[0]) / col_r[pl.ds(0, FB)]
        gro_ref[...] = jnp.sum(t.T, axis=0, keepdims=True) * (1.0 / 64.0)
        t = acc_si[pl.ds(0, FB)] + acc_in[1]
        gsi_ref[...] = jnp.sum(t.T, axis=0, keepdims=True) * (1.0 / 64.0)

    def transpose_w():
        w_in[1].wait_recv()
        w_copies[1].wait()
        for j in range(D // 128):
            cs = pl.ds(j * 128, 128)
            wt[cs, :] = wi[:, cs].astype(F32).T.astype(BF)

    def wait_wo():
        w_in[0].wait_recv()
        w_copies[0].wait()

    DP = D // NH

    def sum_send(step, h):
        rows = pl.ds(h * DP, DP)
        for k in range(3 * step, 3 * step + 3):
            way, _, (ds, dr) = HOPS[k]
            t = slope[ds, rows, pl.ds(dr * TB, TB)]
            for k2 in range(15):
                if HOPS[k2][1] == (ds, dr):
                    t += rbuf[k2, rows].astype(F32)
            sbuf[k, rows] = t.astype(BF)
            send(
                sbuf.at[k, rows], rbuf.at[k, rows], ring_s.at[2, k, h], ring_r.at[2, k, h], (zm, zp, yo)[way]
            )

    def sum_wait(step, h):
        for k in range(3 * step, 3 * step + 3):
            way = HOPS[k][0]
            ref = rbuf.at[k, pl.ds(h * DP, DP)]
            pltpu.make_async_remote_copy(
                src_ref=ref, dst_ref=ref, send_sem=ring_s.at[2, k, h], recv_sem=ring_r.at[2, k, h],
                device_id=(zm, zp, yo)[way], device_id_type=MESH,
            ).wait_recv()

    def col_wait():
        for copy in col_in:
            copy.wait_recv()

    def z_wait():
        for h in range(NH):
            gather_wait(0, z_all, 4, h)

    f = functools.partial
    z_work = [
        [f(gelu, 0, 0), f(gelu, 7, 0)],
        [col_wait, f(gelu, 0, 1)],
        [wait_wo, f(gelu, 7, 1), f(gelu, 1, 0)],
        [f(gelu, 1, 1), f(grad_pre, 0)],
        [f(gelu, 2, 0), f(gelu, 2, 1)],
        [f(gelu, 6, 0), f(grad_pre, 7)],
        [f(gelu, 6, 1), f(gelu, 5, 0)],
        [f(gelu, 5, 1), f(grad_pre, 1)],
        [f(gelu, 3, 0), f(gelu, 3, 1)],
        [f(gelu, 4, 0), f(gelu, 4, 1)],
    ]
    in_work = [
        [f(grad_pre, 2), transpose_w],
        [f(grad_pre, 6), f(grad_h, 6)],
        [z_wait, f(grad_pre, 5), f(grad_h, 5)],
        [f(grad_pre, 3), f(grad_h, 3)],
        [f(grad_pre, 4), f(grad_h, 4), acc_send],
        [f(grad_w, part, hid, z_all, 1, ORDER, True), f(w_sib, 0), f(grad_h, 2)],
        [f(grad_w, gwo_ref, hid, z_all, 0, ORDER, True), f(grad_h, 7)],
        [f(w_x, 0), f(grad_h, 1), f(grad_h, 0)],
        [f(grad_w, part, gp, in_all, 1, ORDER[:3], True), acc_end],
        [f(grad_w, gwi_ref, gp, in_all, 0, ORDER[:3], True), f(w_h, 0)],
    ]
    sum_work = [
        [f(grad_w, part, gp, in_all, 1, ORDER[3:], False), f(w_sib, 1), f(v_part, 1, part)],
        [f(grad_w, gwi_ref, gp, in_all, 0, ORDER[3:], False), f(v_part, 0, gwi_ref), f(v_pair, 0, co)],
        [f(w_x, 1), f(w_all, 0), f(v_sum, 0), f(v_pair, 1, yo)],
        [f(v_sum, 1), f(v_send, 0)],
        [f(w_end, 0)],
        [f(w_h, 1), f(v_wait, 0), f(v_send, 1)],
        [f(v_wait, 1), f(v_send, 2)],
        [f(v_wait, 2), f(v_send, 3)],
        [f(w_all, 1)],
        [f(v_wait, 3), v_end],
    ]

    for step in range(5):
        for h in range(NH):
            if step:
                gather_wait(0, z_all, step - 1, h)
                gather_send(0, z_all, step, h)
            for job in z_work[2 * step + h]:
                job()
    for h in range(NH):
        gather_send(1, in_all, 0, h)
    for step in range(5):
        for h in range(NH):
            if step:
                gather_wait(1, in_all, step - 1, h)
                gather_send(1, in_all, step, h)
            for job in in_work[2 * step + h]:
                job()
    for step in range(5):
        for h in range(NH):
            if step:
                sum_wait(5 - step, h)
            sum_send(4 - step, h)
            if step == 0 and h == 0:
                for hh in range(NH):
                    gather_wait(1, in_all, 4, hh)
            for job in sum_work[2 * step + h]:
                job()
    for h in range(NH):
        sum_wait(0, h)
    for j in range(D // 128):
        cs = pl.ds(j * 128, 128)
        t = slope[0, cs, pl.ds(0, TB)]
        for k in range(3):
            t += rbuf[k, cs].astype(F32)
        gx_ref[:, cs] = t.T * ri_ref[:, cs]
    w_end(1)
    for copy in sent:
        copy.wait_send()


def per_device(
    inputs, cotangent, counts, pre_hidden, pre_out, w_in, w_out, r_in, s_in, r_out, s_out
):
    vm, hbm = pl.BlockSpec(memory_space=pltpu.VMEM), pl.BlockSpec(memory_space=pl.ANY)
    dma = pltpu.SemaphoreType.DMA
    outs = pl.pallas_call(
        kernel,
        out_shape=[
            jax.ShapeDtypeStruct(shape, F32)
            for shape in ((TB, D), (FB, D), (FB, D), (1, D), (1, FB), (1, FB), (1, D))
        ],
        in_specs=[vm, vm, vm, hbm, vm, hbm, hbm, vm, vm, vm, vm],
        out_specs=[vm] * 7,
        scratch_shapes=[
            pltpu.VMEM((NZ, NF, 2 * TB), BF),
            pltpu.VMEM((NZ, NF, 2 * TB), F32),
            pltpu.VMEM((NZ, NF, 2 * TB), BF),
            pltpu.VMEM((NZ, NF, 2 * TB), BF),
            pltpu.VMEM((NZ, 2 * TB, D), BF),
            pltpu.VMEM((NZ, 2 * TB, D), BF),
            pltpu.VMEM((NF, D), BF),
            pltpu.VMEM((NF, D), BF),
            pltpu.VMEM((D, NF), BF),
            pltpu.VMEM((15, D, TB), BF),
            pltpu.VMEM((15, D, TB), BF),
            pltpu.VMEM((NF, 128), F32),
            pltpu.VMEM((NF, 128), F32),
            pltpu.VMEM((2, FB, 128), F32),
            pltpu.VMEM((NF, 128), F32),
            pltpu.VMEM((NF, 128), F32),
            pltpu.VMEM((FB, D), F32),
            pltpu.VMEM((2, FB, D), BF),
            pltpu.VMEM((2, FB, D), BF),
            pltpu.VMEM((2, FB, D), BF),
            pltpu.VMEM((2, 3, 128, D), BF),
            pltpu.VMEM((2, 2, 128, D), BF),
            pltpu.VMEM((2, 4, 128, D), BF),
            pltpu.VMEM((2, 8, D), F32),
            pltpu.VMEM((2, 8, D), F32),
            pltpu.VMEM((NZ, 8, D), F32),
            dma((3, 15, NH)), dma((3, 15, NH)),
            dma((NZ, 2)), dma((NZ, 2)), dma((NZ, 2)),
            dma((2,)), dma((2,)), dma((2,)),
            dma((2,)), dma((2,)),
            dma((2,)), dma((2,)),
            dma((2,)), dma((2,)),
            dma((2, 3)), dma((2, 3)),
            dma((2,)), dma((2,)),
            dma((2, 3)), dma((2, 3)),
            dma((2,)), dma((2,)),
            dma((2, 4)), dma((2, 4)),
        ],
        compiler_params=pltpu.CompilerParams(
            collective_id=0, has_side_effects=True, vmem_limit_bytes=63 * 2**20
        ),
    )(inputs[0], cotangent[0], counts, pre_hidden[0], pre_out[0], w_in, w_out, r_in, s_in, r_out, s_out)
    gx, gwi, gwo, gri, gsi, gro, gso = outs
    return gx[None], gwi, gwo, gri, gsi, gro, gso


def solution(mesh):
    return jax.shard_map(
        per_device,
        mesh=mesh,
        in_specs=(
            P("member", "dp", None),
            P("member", "dp", None),
            P("member", "dp"),
            P("member", "dp", None),
            P("member", "dp", None),
            P("dp", None),
            P("dp", None),
            P("member", None),
            P("member", "dp"),
            P("member", "dp"),
            P("member", None),
        ),
        out_specs=(
            P("member", "dp", None),
            P("dp", None),
            P("dp", None),
            P("member", None),
            P("member", "dp"),
            P("member", "dp"),
            P("member", None),
        ),
        check_vma=False,
    )
```

```python
import functools

import jax
import jax.numpy as jnp
from jax import lax
from jax.experimental import pallas as pl
from jax.experimental.pallas import tpu as pltpu
from jax.sharding import PartitionSpec as P

MESH = pl.DeviceIdType.MESH
BF = jnp.bfloat16
F32 = jnp.float32

NZ = 8
TB = 128
D = 896
FB = 480
NF = 2 * FB
PARTS = (4, 2, 2, 4)
CA = 512
WSCALE = 32768.0**-0.5

HOPS = (
    (0, (0, 0), (7, 0)), (1, (0, 0), (1, 0)), (2, (0, 0), (0, 1)),
    (0, (7, 0), (6, 0)), (1, (1, 0), (2, 0)), (2, (7, 0), (7, 1)),
    (0, (6, 0), (5, 0)), (1, (2, 0), (3, 0)), (2, (1, 0), (1, 1)),
    (0, (5, 0), (4, 0)), (1, (1, 1), (2, 1)), (2, (6, 0), (6, 1)),
    (0, (6, 1), (5, 1)), (1, (2, 1), (3, 1)), (2, (4, 0), (4, 1)),
)
ORDER = (0, 7, 1, 2, 6, 5, 3, 4)


def kernel(
    x_ref, dy_ref, cnt_ref, ph_ref, po_ref, wi_ref, wo_ref, ri_ref, si_ref, ro_ref, so_ref,
    gx_ref, gw_ref, gri_ref, gsi_ref, gro_ref, gso_ref,
    gwi_ref, gwo_ref, pre, slope, hid, gp, z_all, in_all, wo, wi, wt, rbuf, sbuf, acc_ro, acc_si, acc_in,
    col_s, col_r, part, sib_out, sib_in, mem_out, mem_x, mem_h, mem_all, vec_out, vec_in, vec_z,
    ring_s, ring_r, pre_l, pre_s, pre_r, w_l, w_s, w_r, col_ss, col_sr, acc_ss, acc_sr,
    sib_ss, sib_sr, x_s, x_r, h_s, h_r, all_s, all_r, vec_ss, vec_sr, vz_s, vz_r,
):
    m, d = lax.axis_index("member"), lax.axis_index("dp")
    z, y, c = d // 4, (d // 2) % 2, d % 2
    yh, x = m // 4, m % 4
    zp = (m, lax.rem(z + 1, NZ) * 4 + y * 2 + c)
    zm = (m, lax.rem(z + NZ - 1, NZ) * 4 + y * 2 + c)
    yo = (m, z * 4 + (1 - y) * 2 + c)
    co = (m, z * 4 + y * 2 + (1 - c))
    xs = [(yh * 4 + lax.rem(x + k, 4), d) for k in (1, 2, 3)]
    ho = ((1 - yh) * 4 + x, d)
    sent = []

    def send(src, dst, ss, rs, dev):
        copy = pltpu.make_async_remote_copy(
            src_ref=src, dst_ref=dst, send_sem=ss, recv_sem=rs, device_id=dev, device_id_type=MESH
        )
        copy.start()
        sent.append(copy)
        return copy

    barrier = pltpu.get_barrier_semaphore()
    for dev in (zp, zm, yo, co, ho, *xs):
        pl.semaphore_signal(barrier, inc=1, device_id=dev, device_id_type=MESH)

    local = []
    for i, s in enumerate(ORDER):
        zs = lax.rem(z + s, NZ)
        for r in range(2):
            yy = y if r == 0 else 1 - y
            col = pl.multiple_of((zs * 4 + yy * 2 + c) * TB, TB)
            copy = pltpu.make_async_copy(
                ph_ref.at[:, pl.ds(col, TB)], pre.at[s, pl.ds(0, FB), pl.ds(r * TB, TB)], pre_l.at[s, r]
            )
            copy.start()
            local.append(copy)
    w_copies = []
    for i, (src, dst) in enumerate(((wo_ref, wo), (wi_ref, wi))):
        copy = pltpu.make_async_copy(src, dst.at[pl.ds(0, FB)], w_l.at[i])
        copy.start()
        w_copies.append(copy)

    cnt = jnp.broadcast_to(cnt_ref[...].astype(F32), (TB, TB)).T
    for j in range(D // 128):
        cs = pl.ds(j * 128, 128)
        weighted = dy_ref[:, cs].astype(F32) * cnt
        z_all[0, pl.ds(0, TB), cs] = (weighted * so_ref[:, cs]).astype(BF)
        in_all[0, pl.ds(0, TB), cs] = (x_ref[:, cs].astype(F32) * ri_ref[:, cs]).astype(BF)
        vec_out[0, pl.ds(0, 1), cs] = jnp.sum(weighted * po_ref[:, cs].astype(F32), axis=0, keepdims=True)

    pl.semaphore_wait(barrier, 8)

    Z, A, B, R = range(4)
    columns = (pl.ds(0, D), pl.ds(0, CA), pl.ds(CA, D - CA))

    def block(u, at, p):
        rows = TB // PARTS[u]
        return (z_all if u == Z else in_all).at[at[0], pl.ds(at[1] * TB + p * rows, rows), columns[u]]

    def gather_send(u, step, p):
        for k in range(3 * step, 3 * step + 3):
            way, src, dst = HOPS[k]
            send(block(u, src, p), block(u, dst, p), ring_s.at[u, k, p], ring_r.at[u, k, p], (zp, zm, yo)[way])

    def arrived(u, k, p, ref):
        pltpu.make_async_remote_copy(
            src_ref=ref, dst_ref=ref, send_sem=ring_s.at[u, k, p], recv_sem=ring_r.at[u, k, p],
            device_id=yo, device_id_type=MESH,
        ).wait_recv()

    def gather_wait(u, step, p):
        for k in range(3 * step, 3 * step + 3):
            arrived(u, k, p, block(u, HOPS[k][2], p))

    for p in range(PARTS[Z]):
        gather_send(Z, 0, p)

    pre_in = {}
    for s in ORDER:
        zs = lax.rem(z + s, NZ)
        for r in range(2):
            yy = y if r == 0 else 1 - y
            col = pl.multiple_of((zs * 4 + yy * 2 + (1 - c)) * TB, TB)
            pre_in[s, r] = send(
                ph_ref.at[:, pl.ds(col, TB)], pre.at[s, pl.ds(FB, FB), pl.ds(r * TB, TB)],
                pre_s.at[s, r], pre_r.at[s, r], co,
            )
        if s == 0:
            col_s[pl.ds(0, FB)] = jnp.broadcast_to(si_ref[...], (128, FB)).T
            col_r[pl.ds(0, FB)] = jnp.broadcast_to(ro_ref[...], (128, FB)).T
            col_in = [
                send(b.at[pl.ds(0, FB)], b.at[pl.ds(FB, FB)], col_ss.at[i], col_sr.at[i], co)
                for i, b in enumerate((col_s, col_r))
            ]
        if s == 7:
            w_in = [
                send(src, dst.at[pl.ds(FB, FB)], w_s.at[i], w_r.at[i], co)
                for i, (src, dst) in enumerate(((wo_ref, wo), (wi_ref, wi)))
            ]
    vec_out[0, pl.ds(2, 6)] = jnp.zeros((6, D), F32)
    acc_ro[...] = jnp.zeros_like(acc_ro)
    acc_si[...] = jnp.zeros_like(acc_si)

    GT = 32

    def gelu(s, side):
        if side == 0:
            for r in range(2):
                local[2 * ORDER.index(s) + r].wait()
        else:
            for r in range(2):
                pre_in[s, r].wait_recv()

        def tile(i, _):
            rows = pl.ds(pl.multiple_of(side * FB + i * GT, GT), GT)
            sc, rc = col_s[rows], col_r[rows]
            for j in range(2):
                cs = pl.ds(j * 128, 128)
                v = pre[s, rows, cs].astype(F32) * sc
                cdf = 0.5 * (1.0 + lax.erf(v * 0.7071067811865476))
                hid[s, rows, cs] = (v * cdf * rc).astype(BF)
                pdf = jnp.exp(-0.5 * v * v) * 0.3989422804014327
                slope[s, rows, cs] = (cdf + v * pdf) * rc
            return 0

        lax.fori_loop(0, FB // GT, tile, 0)

    UT = 240

    def grad_pre(s, side):
        def tile(i, _):
            rows = pl.ds(pl.multiple_of(side * FB + i * UT, 16), UT)
            u = lax.dot_general(wo[rows], z_all[s], (((1,), (1,)), ((), ())), preferred_element_type=F32)
            sc = col_s[rows]
            q = u * hid[s, rows].astype(F32)
            acc_ro[rows] += q[:, :128] + q[:, 128:]
            a = u * slope[s, rows]
            q = a * pre[s, rows].astype(F32)
            acc_si[rows] += q[:, :128] + q[:, 128:]
            gp[s, rows, pl.ds(0, 128)] = (a[:, :128] * sc).astype(BF)
            gp[s, rows, pl.ds(128, 128)] = (a[:, 128:] * sc).astype(BF)
            return 0

        lax.fori_loop(0, FB // UT, tile, 0)

    HT = 448

    def grad_h(s):
        def tile(i, _):
            rows = pl.ds(pl.multiple_of(i * HT, 16), HT)
            slope[s, rows] = jnp.dot(wt[rows], gp[s], preferred_element_type=F32)
            return 0

        lax.fori_loop(0, D // HT, tile, 0)

    WT = 240

    def grad_w(g, side, slots, first):
        lhs, rhs = (hid, z_all) if g == 0 else (gp, in_all)
        out, cols = (part if side else accs[g]), columns[g]

        def tile(i, _):
            rows = pl.ds(pl.multiple_of(i * WT, 16), WT)
            src = pl.ds(pl.multiple_of(side * FB + i * WT, 16), WT)
            for n, s in enumerate(slots):
                t = jnp.dot(lhs[s, src], rhs[s, :, cols], preferred_element_type=F32)
                if first and n == 0:
                    out[rows, cols] = t
                else:
                    out[rows, cols] += t
            return 0

        lax.fori_loop(0, FB // WT, tile, 0)

    accs = (gwo_ref, gwi_ref, gwi_ref)
    which = (0, 1, 1)
    stage = {}

    def piece(xx):
        return pl.ds(pl.multiple_of(112 * xx + 16 * (xx // 2), 16), 128)

    def w_sib(g):
        a, cols = which[g], columns[g]
        sib_out[a, :, cols] = part[:, cols].astype(BF)
        stage["sib", g] = send(sib_out.at[a, :, cols], sib_in.at[a, :, cols], sib_ss.at[g], sib_sr.at[g], co)

    def w_x(g):
        a, cols = which[g], columns[g]
        stage["sib", g].wait_recv()
        t = accs[g][:, cols] + sib_in[a, :, cols].astype(F32)
        accs[g][:, cols] = t
        mem_out[a, :, cols] = t.astype(BF)
        stage["x", g] = [
            send(
                mem_out.at[a, piece(lax.rem(x + k, 4)), cols], mem_x.at[a, k - 1, :, cols],
                x_s.at[g, k - 1], x_r.at[g, k - 1], xs[k - 1],
            )
            for k in (2, 1, 3)
        ]

    def w_h(g):
        a, cols = which[g], columns[g]
        for copy in stage["x", g]:
            copy.wait_recv()
        total = accs[g][piece(x), cols]
        for k in range(3):
            total += mem_x[a, k, :, cols].astype(F32)
        mem_h[a, 0, :, cols] = total.astype(BF)
        stage["h", g] = send(mem_h.at[a, 0, :, cols], mem_h.at[a, 1, :, cols], h_s.at[g], h_r.at[g], ho)

    def w_all(g):
        a, cols = which[g], columns[g]
        stage["h", g].wait_recv()
        mem_all[a, 0, :, cols] = (mem_h[a, 0, :, cols].astype(F32) + mem_h[a, 1, :, cols].astype(F32)).astype(BF)
        stage["all", g] = [
            send(mem_all.at[a, 0, :, cols], mem_all.at[a, k, :, cols], all_s.at[g, k - 1], all_r.at[g, k - 1], xs[k - 1])
            for k in (2, 1, 3)
        ]

    def w_end(g):
        a, cols = which[g], columns[g]
        for copy in stage["all", g]:
            copy.wait_recv()
        for xx in range(4):
            rows = pl.ds(112 * xx + 16 * (xx // 2), 128)
            gw_ref[a, rows, cols] = mem_all[a, lax.rem(x + 4 - xx, 4), :, cols]

    def v_part(g, side):
        cols, grads = columns[g], part if side else accs[g]
        t = jnp.sum(wi[pl.ds(side * FB, FB), cols].astype(F32) * grads[:, cols], axis=0, keepdims=True)
        if side == 1:
            vec_out[0, pl.ds(1, 1), cols] = t
        else:
            vec_out[0, pl.ds(1, 1), cols] += t

    def v_pair(i, dev):
        stage["v", i] = send(vec_out.at[i], vec_in.at[i], vec_ss.at[i], vec_sr.at[i], dev)

    def v_sum(i):
        stage["v", i].wait_recv()
        t = vec_out[i] + vec_in[i]
        if i == 0:
            vec_out[1] = t
        else:
            vec_z[0] = t

    def v_send(k):
        stage["va", k] = send(vec_z.at[(8 - k) % 8], vec_z.at[7 - k], vz_s.at[0, k], vz_r.at[0, k], zp)
        if k < 3:
            stage["vb", k] = send(vec_z.at[k], vec_z.at[k + 1], vz_s.at[1, k], vz_r.at[1, k], zm)

    def v_wait(k):
        stage["va", k].wait_recv()
        if k < 3:
            stage["vb", k].wait_recv()

    def v_end():
        total = vec_z[lax.rem(NZ - z, NZ)]
        for s in range(1, NZ):
            total += vec_z[lax.rem(s + NZ - z, NZ)]
        gso_ref[...] = total[0:1] * (1.0 / 64.0)
        gri_ref[...] = total[1:2] / ri_ref[...] * (1.0 / 64.0)

    def acc_send():
        stage["acc"] = [
            send(b.at[pl.ds(FB, FB)], acc_in.at[i], acc_ss.at[i], acc_sr.at[i], co)
            for i, b in enumerate((acc_ro, acc_si))
        ]

    def acc_end():
        for copy in stage["acc"]:
            copy.wait_recv()
        t = (acc_ro[pl.ds(0, FB)] + acc_in[0]) / col_r[pl.ds(0, FB)]
        gro_ref[...] = jnp.sum(t.T, axis=0, keepdims=True) * (1.0 / 64.0)
        t = acc_si[pl.ds(0, FB)] + acc_in[1]
        gsi_ref[...] = jnp.sum(t.T, axis=0, keepdims=True) * (1.0 / 64.0)

    def transpose_w():
        w_in[1].wait_recv()
        w_copies[1].wait()
        for j in range(D // 128):
            cs = pl.ds(j * 128, 128)
            wt[cs, :] = wi[:, cs].astype(F32).T.astype(BF)

    def wait_wo():
        w_in[0].wait_recv()
        w_copies[0].wait()

    DP = D // PARTS[R]

    def sum_send(step, p):
        rows = pl.ds(p * DP, DP)
        for k in range(3 * step, 3 * step + 3):
            way, _, (ds, dr) = HOPS[k]
            t = slope[ds, rows, pl.ds(dr * TB, TB)]
            for k2 in range(15):
                if HOPS[k2][1] == (ds, dr):
                    t += rbuf[k2, rows].astype(F32)
            sbuf[k, rows] = t.astype(BF)
            send(sbuf.at[k, rows], rbuf.at[k, rows], ring_s.at[R, k, p], ring_r.at[R, k, p], (zm, zp, yo)[way])

    def sum_wait(step, p):
        for k in range(3 * step, 3 * step + 3):
            arrived(R, k, p, rbuf.at[k, pl.ds(p * DP, DP)])

    def col_wait():
        for copy in col_in:
            copy.wait_recv()

    def gathered(u):
        for p in range(PARTS[u]):
            gather_wait(u, 4, p)

    f = functools.partial
    early, late = ORDER[:5], ORDER[5:]
    plan = (
        (Z, 0, ((f(gelu, 0, 0),), (f(gelu, 7, 0),), (f(gelu, 1, 0),), (f(gelu, 2, 0),))),
        (Z, 1, ((col_wait, f(gelu, 0, 1)), (f(gelu, 7, 1),), (f(gelu, 1, 1),), (wait_wo, f(grad_pre, 0, 0)))),
        (Z, 2, ((f(grad_pre, 0, 1),), (f(gelu, 6, 0), f(gelu, 6, 1)), (f(gelu, 2, 1), f(gelu, 5, 0)), (f(grad_pre, 7, 0),))),
        (A, 0, ((f(grad_pre, 7, 1),), (f(gelu, 5, 1), f(gelu, 3, 0)))),
        (Z, 3, ((f(gelu, 3, 1),), (f(gelu, 4, 0),), (f(gelu, 4, 1),), (f(grad_pre, 1, 0),))),
        (Z, 4, ((f(grad_pre, 1, 1),), (transpose_w,), (f(grad_h, 0),), (f(grad_pre, 2, 0),))),
        (A, 1, ((f(grad_pre, 2, 1),), (f(grad_pre, 6, 0),))),
        (B, 0, ((f(grad_pre, 6, 1),), (f(grad_h, 6),))),
        (A, 2, ((f(gathered, Z), f(grad_w, 0, 1, ORDER[:4], True)), (f(grad_w, 0, 1, ORDER[4:], False), f(w_sib, 0)))),
        (B, 1, ((f(grad_w, 0, 0, ORDER[:4], True),), (f(grad_w, 0, 0, ORDER[4:], False),))),
        (A, 3, ((f(grad_pre, 5, 0),), (f(grad_pre, 5, 1),))),
        (B, 2, ((f(w_x, 0), f(grad_pre, 3, 0)), (f(grad_pre, 3, 1),))),
        (A, 4, ((f(grad_pre, 4, 0),), (f(grad_pre, 4, 1), acc_send))),
        (B, 3, ((f(grad_h, 5), f(grad_h, 3)), (f(grad_h, 4), f(grad_h, 2)))),
        (R, 4, (
            (f(grad_w, 1, 1, early, True),), (f(grad_w, 1, 0, early, True),),
            (f(gathered, A), f(grad_w, 1, 1, late, False), f(w_sib, 1)),
            (f(grad_w, 1, 0, late, False), f(v_part, 1, 1), f(v_part, 1, 0)),
        )),
        (B, 4, ((f(w_x, 1), f(w_h, 0)), (f(grad_w, 2, 1, early, True),))),
        (R, 3, (
            (f(grad_w, 2, 0, early, True),), (f(grad_h, 1),),
            (f(gathered, B), f(grad_w, 2, 1, late, False), f(w_sib, 2)),
            (f(grad_w, 2, 0, late, False), f(v_part, 2, 1), f(v_part, 2, 0)),
        )),
        (R, 2, ((f(w_x, 2), f(v_pair, 0, co)), (f(grad_h, 7), acc_end), (f(w_all, 0), f(v_sum, 0), f(v_pair, 1, yo)), ())),
        (R, 1, ((f(w_h, 1), f(v_sum, 1), f(v_send, 0)), (), (f(v_wait, 0), f(v_send, 1)), (f(w_h, 2),))),
        (R, 0, ((f(w_all, 1), f(v_wait, 1), f(v_send, 2)), (f(w_end, 0),), (f(w_all, 2), f(v_wait, 2), f(v_send, 3)), ())),
    )
    for n, (u, step, work) in enumerate(plan):
        for p in range(PARTS[u]):
            if u == R:
                if step < 4:
                    sum_wait(step + 1, p)
                sum_send(step, p)
            elif n:
                if step:
                    gather_wait(u, step - 1, p)
                gather_send(u, step, p)
            for job in work[p]:
                job()
    w_end(1)
    v_wait(3)
    v_end()
    for p in range(PARTS[R]):
        sum_wait(0, p)
    for j in range(D // 128):
        cs = pl.ds(j * 128, 128)
        t = slope[0, cs, pl.ds(0, TB)]
        for k in range(3):
            t += rbuf[k, cs].astype(F32)
        gx_ref[:, cs] = t.T * ri_ref[:, cs]
    w_end(2)
    for copy in sent:
        copy.wait_send()


def finish(gx, gw, gri, gsi, gro, gso, gx_out, gwi_out, gwo_out, gri_out, gsi_out, gro_out, gso_out):
    gwo_out[...] = gw[0].astype(F32) * WSCALE
    gwi_out[...] = gw[1].astype(F32) * WSCALE

    @pl.when(pl.program_id(0) == 0)
    def _():
        for src, dst in ((gx, gx_out), (gri, gri_out), (gsi, gsi_out), (gro, gro_out), (gso, gso_out)):
            dst[...] = src[...]


def per_device(
    inputs, cotangent, counts, pre_hidden, pre_out, w_in, w_out, r_in, s_in, r_out, s_out
):
    vm, hbm = pl.BlockSpec(memory_space=pltpu.VMEM), pl.BlockSpec(memory_space=pl.ANY)
    dma = pltpu.SemaphoreType.DMA
    shapes = (((TB, D), F32), ((2, FB, D), BF), ((1, D), F32), ((1, FB), F32), ((1, FB), F32), ((1, D), F32))
    outs = pl.pallas_call(
        kernel,
        out_shape=[jax.ShapeDtypeStruct(shape, dtype) for shape, dtype in shapes],
        in_specs=[vm, vm, vm, hbm, vm, hbm, hbm, vm, vm, vm, vm],
        out_specs=[vm] * 6,
        scratch_shapes=[
            pltpu.VMEM((FB, D), F32),
            pltpu.VMEM((FB, D), F32),
            pltpu.VMEM((NZ, NF, 2 * TB), BF),
            pltpu.VMEM((NZ, NF, 2 * TB), F32),
            pltpu.VMEM((NZ, NF, 2 * TB), BF),
            pltpu.VMEM((NZ, NF, 2 * TB), BF),
            pltpu.VMEM((NZ, 2 * TB, D), BF),
            pltpu.VMEM((NZ, 2 * TB, D), BF),
            pltpu.VMEM((NF, D), BF),
            pltpu.VMEM((NF, D), BF),
            pltpu.VMEM((D, NF), BF),
            pltpu.VMEM((15, D, TB), BF),
            pltpu.VMEM((15, D, TB), BF),
            pltpu.VMEM((NF, 128), F32),
            pltpu.VMEM((NF, 128), F32),
            pltpu.VMEM((2, FB, 128), F32),
            pltpu.VMEM((NF, 128), F32),
            pltpu.VMEM((NF, 128), F32),
            pltpu.VMEM((FB, D), F32),
            pltpu.VMEM((2, FB, D), BF),
            pltpu.VMEM((2, FB, D), BF),
            pltpu.VMEM((2, FB, D), BF),
            pltpu.VMEM((2, 3, 128, D), BF),
            pltpu.VMEM((2, 2, 128, D), BF),
            pltpu.VMEM((2, 4, 128, D), BF),
            pltpu.VMEM((2, 8, D), F32),
            pltpu.VMEM((2, 8, D), F32),
            pltpu.VMEM((NZ, 8, D), F32),
            dma((4, 15, 4)), dma((4, 15, 4)),
            dma((NZ, 2)), dma((NZ, 2)), dma((NZ, 2)),
            dma((2,)), dma((2,)), dma((2,)),
            dma((2,)), dma((2,)),
            dma((2,)), dma((2,)),
            dma((3,)), dma((3,)),
            dma((3, 3)), dma((3, 3)),
            dma((3,)), dma((3,)),
            dma((3, 3)), dma((3, 3)),
            dma((2,)), dma((2,)),
            dma((2, 4)), dma((2, 4)),
        ],
        compiler_params=pltpu.CompilerParams(
            collective_id=0, has_side_effects=True, vmem_limit_bytes=63 * 2**20
        ),
    )(inputs[0], cotangent[0], counts, pre_hidden[0], pre_out[0], w_in, w_out, r_in, s_in, r_out, s_out)
    steps = 3

    def whole(shape):
        return pl.BlockSpec(shape, lambda i: (0,) * len(shape))

    rows = pl.BlockSpec((FB // steps, D), lambda i: (i, 0))
    small = [whole(shape) for shape, _ in shapes[2:]]
    gx, gwi, gwo, gri, gsi, gro, gso = pl.pallas_call(
        finish,
        grid=(steps,),
        out_shape=[
            jax.ShapeDtypeStruct(shape, F32)
            for shape in ((TB, D), (FB, D), (FB, D), (1, D), (1, FB), (1, FB), (1, D))
        ],
        in_specs=[whole((TB, D)), pl.BlockSpec((2, FB // steps, D), lambda i: (0, i, 0)), *small],
        out_specs=[whole((TB, D)), rows, rows, *small],
        compiler_params=pltpu.CompilerParams(vmem_limit_bytes=63 * 2**20),
    )(*outs)
    return gx[None], gwi, gwo, gri, gsi, gro, gso


def solution(mesh):
    return jax.shard_map(
        per_device,
        mesh=mesh,
        in_specs=(
            P("member", "dp", None),
            P("member", "dp", None),
            P("member", "dp"),
            P("member", "dp", None),
            P("member", "dp", None),
            P("dp", None),
            P("dp", None),
            P("member", None),
            P("member", "dp"),
            P("member", "dp"),
            P("member", None),
        ),
        out_specs=(
            P("member", "dp", None),
            P("dp", None),
            P("dp", None),
            P("member", None),
            P("member", "dp"),
            P("member", "dp"),
            P("member", None),
        ),
        check_vma=False,
    )
```

```python
import functools

import jax
import jax.numpy as jnp
from jax import lax
from jax.experimental import pallas as pl
from jax.experimental.pallas import tpu as pltpu
from jax.sharding import PartitionSpec as P

MESH = pl.DeviceIdType.MESH
BF = jnp.bfloat16
F32 = jnp.float32

NZ = 8
TB = 128
D = 896
FB = 480
NF = 2 * FB
PARTS = (4, 2, 2, 4)
CA = 512
WSCALE = 32768.0**-0.5

HOPS = (
    (0, (0, 0), (7, 0)), (1, (0, 0), (1, 0)), (2, (0, 0), (0, 1)),
    (0, (7, 0), (6, 0)), (1, (1, 0), (2, 0)), (2, (7, 0), (7, 1)),
    (0, (6, 0), (5, 0)), (1, (2, 0), (3, 0)), (2, (1, 0), (1, 1)),
    (0, (5, 0), (4, 0)), (1, (1, 1), (2, 1)), (2, (6, 0), (6, 1)),
    (0, (6, 1), (5, 1)), (1, (2, 1), (3, 1)), (2, (4, 0), (4, 1)),
)
LAST = ((0, (5, 1), (4, 1)), (0, (5, 1), (4, 1)), (1, (3, 1), (4, 1)), (1, (3, 1), (4, 1)))
SUM_STEPS = ((0, 1, 2), (3, 4), (6, 7, 8), (9, 10, 11), (12, 13), (14, 5))
SUM_ROWS = ((0, 256), (256, 256), (512, 256), (768, 128))
ORDER = (0, 7, 1, 2, 6, 5, 3, 4)


def kernel(
    x_hbm, dy_hbm, cnt_ref, ph_ref, po_hbm, wi_ref, wo_ref, ri_ref, si_ref, ro_ref, so_ref,
    gx_ref, gw_ref, gri_ref, gsi_ref, gro_ref, gso_ref,
    x_ref, dy_ref, po_ref, own_l, gwi_ref, gwo_ref, pre, slope, hid, gp, z_all, in_all, wo, wi, wt, rbuf, sbuf, acc_ro, acc_si, acc_in,
    col_s, col_r, part, sib_out, sib_in, mem_out, mem_x, mem_h, mem_all, vec_out, vec_in, vec_z,
    ring_s, ring_r, pre_l, pre_s, pre_r, w_l, w_s, w_r, col_ss, col_sr, acc_ss, acc_sr,
    sib_ss, sib_sr, x_s, x_r, h_s, h_r, all_s, all_r, vec_ss, vec_sr, vz_s, vz_r,
):
    m, d = lax.axis_index("member"), lax.axis_index("dp")
    z, y, c = d // 4, (d // 2) % 2, d % 2
    yh, x = m // 4, m % 4
    zp = (m, lax.rem(z + 1, NZ) * 4 + y * 2 + c)
    zm = (m, lax.rem(z + NZ - 1, NZ) * 4 + y * 2 + c)
    yo = (m, z * 4 + (1 - y) * 2 + c)
    co = (m, z * 4 + y * 2 + (1 - c))
    xs = [(yh * 4 + lax.rem(x + k, 4), d) for k in (1, 2, 3)]
    ho = ((1 - yh) * 4 + x, d)
    zs_all = [(m, lax.rem(z + k, NZ) * 4 + y * 2 + c) for k in range(1, NZ)]
    sent = []

    def send(src, dst, ss, rs, dev):
        copy = pltpu.make_async_remote_copy(
            src_ref=src, dst_ref=dst, send_sem=ss, recv_sem=rs, device_id=dev, device_id_type=MESH
        )
        copy.start()
        sent.append(copy)
        return copy

    barrier = pltpu.get_barrier_semaphore()
    for dev in (yo, co, ho, *xs, *zs_all):
        pl.semaphore_signal(barrier, inc=1, device_id=dev, device_id_type=MESH)

    own = [
        pltpu.make_async_copy(src, dst, own_l.at[i])
        for i, (src, dst) in enumerate(((dy_hbm, dy_ref), (x_hbm, x_ref), (po_hbm, po_ref)))
    ]
    for copy in own:
        copy.start()
    w_copies = []
    for i, (src, dst) in enumerate(((wo_ref, wo), (wi_ref, wi))):
        copy = pltpu.make_async_copy(src, dst.at[pl.ds(0, FB)], w_l.at[i])
        copy.start()
        w_copies.append(copy)

    cnt = jnp.broadcast_to(cnt_ref[...].astype(F32), (TB, TB)).T
    own[0].wait()
    for j in range(D // 128):
        cs = pl.ds(j * 128, 128)
        z_all[0, pl.ds(0, TB), cs] = (dy_ref[:, cs].astype(F32) * cnt * so_ref[:, cs]).astype(BF)

    pl.semaphore_wait(barrier, 13)

    Z, A, B, R = range(4)
    columns = (pl.ds(0, D), pl.ds(0, CA), pl.ds(CA, D - CA))

    def block(u, at, p):
        rows = TB // PARTS[u]
        return (z_all if u == Z else in_all).at[at[0], pl.ds(at[1] * TB + p * rows, rows), columns[u]]

    def gather_send(u, step, p):
        for k in range(3 * step, 3 * step + 3):
            way, src, dst = HOPS[k]
            for k2 in range(15):
                if HOPS[k2][2] == src:
                    need(u, k2, p)
            send(block(u, src, p), block(u, dst, p), ring_s.at[u, k, p], ring_r.at[u, k, p], (zp, zm, yo)[way])

    done = set()

    def need(u, k, p):
        if (u, k, p) in done:
            return
        done.add((u, k, p))
        ref = rbuf.at[k, pl.ds(*SUM_ROWS[p])] if u == R else block(u, HOPS[k][2], p)
        pltpu.make_async_remote_copy(
            src_ref=ref, dst_ref=ref, send_sem=ring_s.at[u, k, p], recv_sem=ring_r.at[u, k, p],
            device_id=yo, device_id_type=MESH,
        ).wait_recv()

    def need_slots(u, slots):
        for k, hop in enumerate(HOPS):
            if hop[2][0] in slots:
                for p in range(PARTS[u]):
                    need(u, k, p)

    for p in range(PARTS[Z]):
        gather_send(Z, 0, p)
    own[1].wait()
    own[2].wait()
    for j in range(D // 128):
        cs = pl.ds(j * 128, 128)
        weighted = dy_ref[:, cs].astype(F32) * cnt
        in_all[0, pl.ds(0, TB), cs] = (x_ref[:, cs].astype(F32) * ri_ref[:, cs]).astype(BF)
        vec_out[0, pl.ds(j, 1)] = jnp.sum(weighted * po_ref[:, cs].astype(F32), axis=0, keepdims=True)

    def patches(s, r, core):
        zs = lax.rem(z + s, NZ)
        yy = y if r == 0 else 1 - y
        return ph_ref.at[:, pl.ds(pl.multiple_of((zs * 4 + yy * 2 + core) * TB, TB), TB)]

    local, pre_in = {}, {}
    for s in ORDER:
        for r in range(2):
            local[s, r] = pltpu.make_async_copy(
                patches(s, r, c), pre.at[s, pl.ds(0, FB), pl.ds(r * TB, TB)], pre_l.at[s, r]
            )
            local[s, r].start()

    def pre_send(s):
        for r in range(2):
            pre_in[s, r] = send(
                patches(s, r, 1 - c), pre.at[s, pl.ds(FB, FB), pl.ds(r * TB, TB)],
                pre_s.at[s, r], pre_r.at[s, r], co,
            )

    w_in = {}

    def w_send(i):
        src, dst = ((wo_ref, wo), (wi_ref, wi))[i]
        w_in[i] = send(src, dst.at[pl.ds(FB, FB)], w_s.at[i], w_r.at[i], co)

    pre_send(0)
    col_s[pl.ds(0, FB)] = jnp.broadcast_to(si_ref[...], (128, FB)).T
    col_r[pl.ds(0, FB)] = jnp.broadcast_to(ro_ref[...], (128, FB)).T
    col_in = [
        send(b.at[pl.ds(0, FB)], b.at[pl.ds(FB, FB)], col_ss.at[i], col_sr.at[i], co)
        for i, b in enumerate((col_s, col_r))
    ]
    vec_out[0, pl.ds(7, 1)] = jnp.zeros((1, 128), F32)
    vec_out[0, pl.ds(15, 1)] = jnp.zeros((1, 128), F32)
    acc_ro[...] = jnp.zeros_like(acc_ro)
    acc_si[...] = jnp.zeros_like(acc_si)

    GT = 32

    def gelu(s, side):
        if side == 0:
            for r in range(2):
                local[s, r].wait()
        else:
            for r in range(2):
                pre_in[s, r].wait_recv()

        def tile(i, _):
            rows = pl.ds(pl.multiple_of(side * FB + i * GT, GT), GT)
            sc, rc = col_s[rows], col_r[rows]
            for j in range(2):
                cs = pl.ds(j * 128, 128)
                v = pre[s, rows, cs].astype(F32) * sc
                cdf = 0.5 * (1.0 + lax.erf(v * 0.7071067811865476))
                hid[s, rows, cs] = (v * cdf * rc).astype(BF)
                pdf = jnp.exp(-0.5 * v * v) * 0.3989422804014327
                slope[s, rows, cs] = (cdf + v * pdf) * rc
            return 0

        lax.fori_loop(0, FB // GT, tile, 0)

    UT = 240

    def grad_pre(s, side):
        need_slots(Z, (s,))

        def tile(i, _):
            rows = pl.ds(pl.multiple_of(side * FB + i * UT, 16), UT)
            u = lax.dot_general(wo[rows], z_all[s], (((1,), (1,)), ((), ())), preferred_element_type=F32)
            sc = col_s[rows]
            q = u * hid[s, rows].astype(F32)
            acc_ro[rows] += q[:, :128] + q[:, 128:]
            a = u * slope[s, rows]
            q = a * pre[s, rows].astype(F32)
            acc_si[rows] += q[:, :128] + q[:, 128:]
            gp[s, rows, pl.ds(0, 128)] = (a[:, :128] * sc).astype(BF)
            gp[s, rows, pl.ds(128, 128)] = (a[:, 128:] * sc).astype(BF)
            return 0

        lax.fori_loop(0, FB // UT, tile, 0)

    HT = 448

    def grad_h(s):
        def tile(i, _):
            rows = pl.ds(pl.multiple_of(i * HT, 16), HT)
            slope[s, rows] = jnp.dot(wt[rows], gp[s], preferred_element_type=F32)
            return 0

        lax.fori_loop(0, D // HT, tile, 0)

    WT = 240

    def grad_w(g, side, slots, first):
        lhs, rhs = (hid, z_all) if g == 0 else (gp, in_all)
        out, cols = (part if side else accs[g]), columns[g]
        need_slots(g, slots)

        def tile(i, _):
            rows = pl.ds(pl.multiple_of(i * WT, 16), WT)
            src = pl.ds(pl.multiple_of(side * FB + i * WT, 16), WT)
            for n, s in enumerate(slots):
                t = jnp.dot(lhs[s, src], rhs[s, :, cols], preferred_element_type=F32)
                if first and n == 0:
                    out[rows, cols] = t
                else:
                    out[rows, cols] += t
            return 0

        lax.fori_loop(0, FB // WT, tile, 0)

    accs = (gwo_ref, gwi_ref, gwi_ref)
    which = (0, 1, 1)
    stage = {}

    def piece(xx):
        return pl.ds(pl.multiple_of(112 * xx + 16 * (xx // 2), 16), 128)

    def w_sib(g):
        a, cols = which[g], columns[g]
        sib_out[a, :, cols] = part[:, cols].astype(BF)
        stage["sib", g] = send(sib_out.at[a, :, cols], sib_in.at[a, :, cols], sib_ss.at[g], sib_sr.at[g], co)

    def w_x(g):
        a, cols = which[g], columns[g]
        stage["sib", g].wait_recv()
        t = accs[g][:, cols] + sib_in[a, :, cols].astype(F32)
        accs[g][:, cols] = t
        mem_out[a, :, cols] = t.astype(BF)
        stage["x", g] = [
            send(
                mem_out.at[a, piece(lax.rem(x + k, 4)), cols], mem_x.at[a, k - 1, :, cols],
                x_s.at[g, k - 1], x_r.at[g, k - 1], xs[k - 1],
            )
            for k in (2, 1, 3)
        ]

    def w_h(g):
        a, cols = which[g], columns[g]
        for copy in stage["x", g]:
            copy.wait_recv()
        total = accs[g][piece(x), cols]
        for k in range(3):
            total += mem_x[a, k, :, cols].astype(F32)
        mem_h[a, 0, :, cols] = total.astype(BF)
        stage["h", g] = send(mem_h.at[a, 0, :, cols], mem_h.at[a, 1, :, cols], h_s.at[g], h_r.at[g], ho)

    def w_all(g):
        a, cols = which[g], columns[g]
        stage["h", g].wait_recv()
        mem_all[a, 0, :, cols] = (mem_h[a, 0, :, cols].astype(F32) + mem_h[a, 1, :, cols].astype(F32)).astype(BF)
        stage["all", g] = [
            send(mem_all.at[a, 0, :, cols], mem_all.at[a, k, :, cols], all_s.at[g, k - 1], all_r.at[g, k - 1], xs[k - 1])
            for k in (2, 1, 3)
        ]

    def w_end(g):
        a, cols = which[g], columns[g]
        for copy in stage["all", g]:
            copy.wait_recv()
        for xx in range(4):
            rows = pl.ds(112 * xx + 16 * (xx // 2), 128)
            gw_ref[a, rows, cols] = mem_all[a, lax.rem(x + 4 - xx, 4), :, cols]

    def v_part(g, side):
        grads = part if side else accs[g]
        for j in range(CA // 128) if g == 1 else range(CA // 128, D // 128):
            cs = pl.ds(j * 128, 128)
            t = jnp.sum(wi[pl.ds(side * FB, FB), cs].astype(F32) * grads[:, cs], axis=0, keepdims=True)
            if side == 1:
                vec_out[0, pl.ds(8 + j, 1)] = t
            else:
                vec_out[0, pl.ds(8 + j, 1)] += t

    def v_pair(i, dev):
        stage["v", i] = send(vec_out.at[i], vec_in.at[i], vec_ss.at[i], vec_sr.at[i], dev)

    def v_sum(i):
        stage["v", i].wait_recv()
        t = vec_out[i] + vec_in[i]
        if i == 0:
            vec_out[1] = t
        else:
            vec_z[0] = t

    def v_send():
        stage["vz"] = [
            send(vec_z.at[0], vec_z.at[NZ - k], vz_s.at[k - 1], vz_r.at[k - 1], zs_all[k - 1]) for k in range(1, NZ)
        ]

    def v_end():
        for copy in stage["vz"]:
            copy.wait_recv()
        total = vec_z[lax.rem(NZ - z, NZ)]
        for s in range(1, NZ):
            total += vec_z[lax.rem(s + NZ - z, NZ)]
        for j in range(D // 128):
            cs = pl.ds(j * 128, 128)
            gso_ref[:, cs] = total[j:j + 1] * (1.0 / 64.0)
            gri_ref[:, cs] = total[8 + j:9 + j] / ri_ref[:, cs] * (1.0 / 64.0)

    def acc_send():
        stage["acc"] = [
            send(b.at[pl.ds(FB, FB)], acc_in.at[i], acc_ss.at[i], acc_sr.at[i], co)
            for i, b in enumerate((acc_ro, acc_si))
        ]

    def acc_end():
        for copy in stage["acc"]:
            copy.wait_recv()
        t = (acc_ro[pl.ds(0, FB)] + acc_in[0]) / col_r[pl.ds(0, FB)]
        gro_ref[...] = jnp.sum(t.T, axis=0, keepdims=True) * (1.0 / 64.0)
        t = acc_si[pl.ds(0, FB)] + acc_in[1]
        gsi_ref[...] = jnp.sum(t.T, axis=0, keepdims=True) * (1.0 / 64.0)

    def transpose_w():
        w_in[1].wait_recv()
        w_copies[1].wait()
        for j in range(D // 128):
            cs = pl.ds(j * 128, 128)
            wt[cs, :] = wi[:, cs].astype(F32).T.astype(BF)

    def wait_wo():
        w_in[0].wait_recv()
        w_copies[0].wait()

    def sum_send(step, p):
        rows = pl.ds(*SUM_ROWS[p])
        hops = (*HOPS[:14], LAST[p])
        for k in SUM_STEPS[step]:
            way, _, (ds, dr) = hops[k]
            t = slope[ds, rows, pl.ds(dr * TB, TB)]
            for k2 in range(15):
                if hops[k2][1] == (ds, dr):
                    need(R, k2, p)
                    t += rbuf[k2, rows].astype(F32)
            sbuf[k, rows] = t.astype(BF)
            send(sbuf.at[k, rows], rbuf.at[k, rows], ring_s.at[R, k, p], ring_r.at[R, k, p], (zm, zp, yo)[way])

    def col_wait():
        for copy in col_in:
            copy.wait_recv()

    f = functools.partial
    early, late = ORDER[:5], ORDER[5:]
    plan = (
        (Z, 0, 0, f(pre_send, 7), f(gelu, 0, 0)),
        (Z, 0, 1, f(w_send, 0), f(gelu, 7, 0)),
        (Z, 0, 2, f(pre_send, 1), f(gelu, 1, 0)),
        (Z, 0, 3, f(pre_send, 2), f(gelu, 2, 0)),
        (Z, 1, 0, f(pre_send, 6), col_wait, f(gelu, 0, 1)),
        (Z, 1, 1, f(w_send, 1), f(gelu, 7, 1)),
        (Z, 1, 2, f(pre_send, 5), f(gelu, 1, 1)),
        (Z, 1, 3, wait_wo, f(grad_pre, 0, 0)),
        (Z, 2, 0, f(pre_send, 3), f(grad_pre, 0, 1)),
        (Z, 2, 1, f(pre_send, 4), f(gelu, 6, 0), f(gelu, 6, 1)),
        (Z, 2, 2, f(gelu, 2, 1), f(gelu, 5, 0)),
        (Z, 2, 3, f(grad_pre, 7, 0)),
        (A, 0, 0, f(grad_pre, 7, 1)),
        (A, 0, 1, f(gelu, 5, 1), f(gelu, 3, 0)),
        (Z, 3, 0, f(gelu, 3, 1)),
        (Z, 3, 1, f(gelu, 4, 0)),
        (Z, 3, 2, f(gelu, 4, 1)),
        (Z, 3, 3, f(grad_pre, 1, 0)),
        (Z, 4, 0, f(grad_pre, 1, 1)),
        (Z, 4, 1, f(grad_w, 0, 1, ORDER[:3], True)),
        (Z, 4, 2, f(grad_w, 0, 0, ORDER[:3], True)),
        (Z, 4, 3, f(grad_pre, 2, 0)),
        (A, 1, 0, transpose_w, f(grad_pre, 2, 1)),
        (A, 1, 1, f(grad_w, 0, 1, (2, 6), False)),
        (B, 0, 0, f(grad_w, 0, 1, late, False), f(w_sib, 0)),
        (B, 0, 1, f(grad_w, 0, 0, (2, 6, *late), False)),
        (A, 2, 0, f(grad_pre, 6, 0)),
        (A, 2, 1, f(w_x, 0), f(grad_pre, 6, 1)),
        (B, 1, 0, f(grad_pre, 5, 0)),
        (B, 1, 1, f(grad_pre, 5, 1)),
        (A, 3, 0, f(grad_pre, 3, 0)),
        (A, 3, 1, f(grad_pre, 3, 1)),
        (B, 2, 0, f(grad_pre, 4, 0)),
        (B, 2, 1, f(grad_pre, 4, 1), acc_send),
        (A, 4, 0, f(grad_h, 4), f(grad_h, 7)),
        (A, 4, 1, f(grad_h, 5), f(grad_h, 3)),
        (B, 3, 0, f(grad_w, 1, 1, early, True)),
        (B, 3, 1, f(w_h, 0), f(grad_w, 1, 0, early, True)),
        (R, 5, 0, f(grad_h, 2)),
        (R, 5, 1, f(grad_w, 1, 1, late, False), f(w_sib, 1)),
        (R, 5, 2, f(grad_w, 1, 0, late, False), f(v_part, 1, 1)),
        (R, 5, 3, f(v_part, 1, 0), f(grad_h, 6)),
        (R, 4, 0, f(w_x, 1)),
        (R, 4, 1, f(grad_h, 1)),
        (B, 4, 0),
        (B, 4, 1, f(grad_w, 2, 1, early, True)),
        (R, 4, 2, f(w_all, 0), f(grad_w, 2, 0, early, True)),
        (R, 4, 3, f(grad_h, 0)),
        (R, 3, 0, f(grad_w, 2, 1, late, False), f(w_sib, 2)),
        (R, 3, 1, f(grad_w, 2, 0, late, False), f(v_part, 2, 1), f(v_part, 2, 0)),
        (R, 3, 2, f(w_x, 2), f(v_pair, 0, co)),
        (R, 3, 3, f(w_h, 1)),
        (R, 2, 0, f(v_sum, 0), f(v_pair, 1, yo)),
        (R, 2, 1, acc_end),
        (R, 2, 2),
        (R, 2, 3, f(w_all, 1)),
        (R, 1, 0, f(v_sum, 1), v_send),
        (R, 1, 1),
        (R, 1, 2, f(w_h, 2)),
        (R, 1, 3),
        (R, 0, 0),
        (R, 0, 1, f(w_end, 0)),
        (R, 0, 2),
        (R, 0, 3, f(w_all, 2), v_end, f(w_end, 1)),
    )
    marks = [len(sent)]
    for n, (u, step, p, *work) in enumerate(plan):
        if u == R:
            sum_send(step, p)
        elif n >= PARTS[Z]:
            gather_send(u, step, p)
        for job in work:
            job()
        marks.append(len(sent))
        if n >= 16:
            for copy in sent[marks[n - 16]:marks[n - 15]]:
                copy.wait_send()
    for p in range(PARTS[R]):
        for k in range(3):
            need(R, k, p)
        at, size = SUM_ROWS[p]
        for j in range(at, at + size, 128):
            cs = pl.ds(j, 128)
            t = slope[0, cs, pl.ds(0, TB)]
            for k in range(3):
                t += rbuf[k, cs].astype(F32)
            gx_ref[:, cs] = t.T * ri_ref[:, cs]
    for copy in (*sent[:marks[0]], *sent[marks[len(plan) - 16]:]):
        copy.wait_send()
    w_end(2)


def finish(gx, gw, gri, gsi, gro, gso, gx_out, gwi_out, gwo_out, gri_out, gsi_out, gro_out, gso_out):
    gwo_out[...] = gw[0].astype(F32) * WSCALE
    gwi_out[...] = gw[1].astype(F32) * WSCALE
    gx_out[...] = gx[...]

    @pl.when(pl.program_id(0) == 0)
    def _():
        for src, dst in ((gri, gri_out), (gsi, gsi_out), (gro, gro_out), (gso, gso_out)):
            dst[...] = src[...]


def per_device(
    inputs, cotangent, counts, pre_hidden, pre_out, w_in, w_out, r_in, s_in, r_out, s_out
):
    vm, hbm = pl.BlockSpec(memory_space=pltpu.VMEM), pl.BlockSpec(memory_space=pl.ANY)
    dma = pltpu.SemaphoreType.DMA
    shapes = (((TB, D), F32), ((2, FB, D), BF), ((1, D), F32), ((1, FB), F32), ((1, FB), F32), ((1, D), F32))
    outs = pl.pallas_call(
        kernel,
        out_shape=[jax.ShapeDtypeStruct(shape, dtype) for shape, dtype in shapes],
        in_specs=[hbm, hbm, vm, hbm, hbm, hbm, hbm, vm, vm, vm, vm],
        out_specs=[vm] * 6,
        scratch_shapes=[
            *[pltpu.VMEM((TB, D), BF)] * 3,
            dma((3,)),
            pltpu.VMEM((FB, D), F32),
            pltpu.VMEM((FB, D), F32),
            pltpu.VMEM((NZ, NF, 2 * TB), BF),
            pltpu.VMEM((NZ, NF, 2 * TB), F32),
            pltpu.VMEM((NZ, NF, 2 * TB), BF),
            pltpu.VMEM((NZ, NF, 2 * TB), BF),
            pltpu.VMEM((NZ, 2 * TB, D), BF),
            pltpu.VMEM((NZ, 2 * TB, D), BF),
            pltpu.VMEM((NF, D), BF),
            pltpu.VMEM((NF, D), BF),
            pltpu.VMEM((D, NF), BF),
            pltpu.VMEM((15, D, TB), BF),
            pltpu.VMEM((15, D, TB), BF),
            pltpu.VMEM((NF, 128), F32),
            pltpu.VMEM((NF, 128), F32),
            pltpu.VMEM((2, FB, 128), F32),
            pltpu.VMEM((NF, 128), F32),
            pltpu.VMEM((NF, 128), F32),
            pltpu.VMEM((FB, D), F32),
            pltpu.VMEM((2, FB, D), BF),
            pltpu.VMEM((2, FB, D), BF),
            pltpu.VMEM((2, FB, D), BF),
            pltpu.VMEM((2, 3, 128, D), BF),
            pltpu.VMEM((2, 2, 128, D), BF),
            pltpu.VMEM((2, 4, 128, D), BF),
            pltpu.VMEM((2, 16, 128), F32),
            pltpu.VMEM((2, 16, 128), F32),
            pltpu.VMEM((NZ, 16, 128), F32),
            dma((4, 15, 4)), dma((4, 15, 4)),
            dma((NZ, 2)), dma((NZ, 2)), dma((NZ, 2)),
            dma((2,)), dma((2,)), dma((2,)),
            dma((2,)), dma((2,)),
            dma((2,)), dma((2,)),
            dma((3,)), dma((3,)),
            dma((3, 3)), dma((3, 3)),
            dma((3,)), dma((3,)),
            dma((3, 3)), dma((3, 3)),
            dma((2,)), dma((2,)),
            dma((7,)), dma((7,)),
        ],
        compiler_params=pltpu.CompilerParams(
            collective_id=0, has_side_effects=True, vmem_limit_bytes=63 * 2**20
        ),
    )(inputs[0], cotangent[0], counts, pre_hidden[0], pre_out[0], w_in, w_out, r_in, s_in, r_out, s_out)
    steps = 3
    rows = pl.BlockSpec((FB // steps, D), lambda i: (i, 0))
    some = pl.BlockSpec((TB // 2, D), lambda i: (jnp.minimum(i, 1), 0))
    small = [pl.BlockSpec(shape, lambda i: (0, 0)) for shape, _ in shapes[2:]]
    gx, gwi, gwo, gri, gsi, gro, gso = pl.pallas_call(
        finish,
        grid=(steps,),
        out_shape=[
            jax.ShapeDtypeStruct(shape, F32)
            for shape in ((TB, D), (FB, D), (FB, D), (1, D), (1, FB), (1, FB), (1, D))
        ],
        in_specs=[some, pl.BlockSpec((2, FB // steps, D), lambda i: (0, i, 0)), *small],
        out_specs=[some, rows, rows, *small],
        compiler_params=pltpu.CompilerParams(vmem_limit_bytes=63 * 2**20),
    )(*outs)
    return gx[None], gwi, gwo, gri, gsi, gro, gso


def solution(mesh):
    return jax.shard_map(
        per_device,
        mesh=mesh,
        in_specs=(
            P("member", "dp", None),
            P("member", "dp", None),
            P("member", "dp"),
            P("member", "dp", None),
            P("member", "dp", None),
            P("dp", None),
            P("dp", None),
            P("member", None),
            P("member", "dp"),
            P("member", "dp"),
            P("member", None),
        ),
        out_specs=(
            P("member", "dp", None),
            P("dp", None),
            P("dp", None),
            P("member", None),
            P("member", "dp"),
            P("member", "dp"),
            P("member", None),
        ),
        check_vma=False,
    )
```

```python
import functools

import jax
import jax.numpy as jnp
from jax import lax
from jax.experimental import pallas as pl
from jax.experimental.pallas import tpu as pltpu
from jax.sharding import PartitionSpec as P

MESH = pl.DeviceIdType.MESH
BF = jnp.bfloat16
F32 = jnp.float32

NZ = 8
TB = 128
D = 896
FB = 480
NF = 2 * FB
PARTS = (4, 2, 2, 4)
CA = 512
WSCALE = 32768.0**-0.5

HOPS = (
    (0, (0, 0), (7, 0)), (1, (0, 0), (1, 0)), (2, (0, 0), (0, 1)),
    (0, (7, 0), (6, 0)), (1, (1, 0), (2, 0)), (2, (7, 0), (7, 1)),
    (0, (6, 0), (5, 0)), (1, (2, 0), (3, 0)), (2, (1, 0), (1, 1)),
    (0, (5, 0), (4, 0)), (1, (1, 1), (2, 1)), (2, (6, 0), (6, 1)),
    (0, (6, 1), (5, 1)), (1, (2, 1), (3, 1)), (2, (4, 0), (4, 1)),
)
LAST = ((0, (5, 1), (4, 1)), (0, (5, 1), (4, 1)), (1, (3, 1), (4, 1)), (1, (3, 1), (4, 1)))
SUM_STEPS = ((0, 1, 2), (3, 4), (6, 7, 8), (9, 10, 11), (12, 13), (14, 5))
SUM_ROWS = ((0, 256), (256, 256), (512, 256), (768, 128))
ORDER = (0, 7, 1, 2, 6, 5, 3, 4)


def kernel(
    x_hbm, dy_hbm, cnt_ref, ph_ref, po_hbm, wi_ref, wo_ref, ri_ref, si_ref, ro_ref, so_ref,
    gx_ref, gw_ref, gri_ref, gsi_ref, gro_ref, gso_ref,
    x_ref, dy_ref, po_ref, own_l, gwi_ref, gwo_ref, pre, slope, hid, gp, z_all, in_all, wo, wi, wt, rbuf, sbuf, acc_ro, acc_si, acc_in,
    col_s, col_r, part, sib_out, sib_in, mem_out, mem_x, mem_h, mem_all, vec_out, vec_in, vec_z,
    ring_s, ring_r, pre_l, pre_s, pre_r, w_l, w_s, w_r, col_ss, col_sr, acc_ss, acc_sr,
    sib_ss, sib_sr, x_s, x_r, h_s, h_r, all_s, all_r, vec_ss, vec_sr, vz_s, vz_r,
):
    m, d = lax.axis_index("member"), lax.axis_index("dp")
    z, y, c = d // 4, (d // 2) % 2, d % 2
    yh, x = m // 4, m % 4
    zp = (m, lax.rem(z + 1, NZ) * 4 + y * 2 + c)
    zm = (m, lax.rem(z + NZ - 1, NZ) * 4 + y * 2 + c)
    yo = (m, z * 4 + (1 - y) * 2 + c)
    co = (m, z * 4 + y * 2 + (1 - c))
    xs = [(yh * 4 + lax.rem(x + k, 4), d) for k in (1, 2, 3)]
    ho = ((1 - yh) * 4 + x, d)
    zs_all = [(m, lax.rem(z + k, NZ) * 4 + y * 2 + c) for k in range(1, NZ)]
    sent = []

    def send(src, dst, ss, rs, dev):
        copy = pltpu.make_async_remote_copy(
            src_ref=src, dst_ref=dst, send_sem=ss, recv_sem=rs, device_id=dev, device_id_type=MESH
        )
        copy.start()
        sent.append(copy)
        return copy

    barrier = pltpu.get_barrier_semaphore()
    for dev in (yo, co, ho, *xs, *zs_all):
        pl.semaphore_signal(barrier, inc=1, device_id=dev, device_id_type=MESH)

    own = [
        pltpu.make_async_copy(src, dst, own_l.at[i])
        for i, (src, dst) in enumerate(((dy_hbm, dy_ref), (x_hbm, x_ref), (po_hbm, po_ref)))
    ]
    for copy in own:
        copy.start()
    w_copies = []
    for i, (src, dst) in enumerate(((wo_ref, wo), (wi_ref, wi))):
        copy = pltpu.make_async_copy(src, dst.at[pl.ds(0, FB)], w_l.at[i])
        copy.start()
        w_copies.append(copy)

    cnt = jnp.broadcast_to(cnt_ref[...].astype(F32), (TB, TB)).T
    own[0].wait()
    for j in range(D // 128):
        cs = pl.ds(j * 128, 128)
        z_all[0, pl.ds(0, TB), cs] = (dy_ref[:, cs].astype(F32) * cnt * so_ref[:, cs]).astype(BF)

    pl.semaphore_wait(barrier, 13)

    Z, A, B, R = range(4)
    columns = (pl.ds(0, D), pl.ds(0, CA), pl.ds(CA, D - CA))

    def block(u, at, p):
        rows = TB // PARTS[u]
        return (z_all if u == Z else in_all).at[at[0], pl.ds(at[1] * TB + p * rows, rows), columns[u]]

    def gather_send(u, step, p):
        for k in range(3 * step, 3 * step + 3):
            way, src, dst = HOPS[k]
            for k2 in range(15):
                if HOPS[k2][2] == src:
                    need(u, k2, p)
            send(block(u, src, p), block(u, dst, p), ring_s.at[u, k, p], ring_r.at[u, k, p], (zp, zm, yo)[way])

    done = set()

    def need(u, k, p):
        if (u, k, p) in done:
            return
        done.add((u, k, p))
        ref = rbuf.at[k, pl.ds(*SUM_ROWS[p])] if u == R else block(u, HOPS[k][2], p)
        pltpu.make_async_remote_copy(
            src_ref=ref, dst_ref=ref, send_sem=ring_s.at[u, k, p], recv_sem=ring_r.at[u, k, p],
            device_id=yo, device_id_type=MESH,
        ).wait_recv()

    def need_slots(u, slots):
        for k, hop in enumerate(HOPS):
            if hop[2][0] in slots:
                for p in range(PARTS[u]):
                    need(u, k, p)

    for p in range(PARTS[Z]):
        gather_send(Z, 0, p)
    own[1].wait()
    own[2].wait()
    for j in range(D // 128):
        cs = pl.ds(j * 128, 128)
        weighted = dy_ref[:, cs].astype(F32) * cnt
        in_all[0, pl.ds(0, TB), cs] = (x_ref[:, cs].astype(F32) * ri_ref[:, cs]).astype(BF)
        vec_out[0, pl.ds(j, 1)] = jnp.sum(weighted * po_ref[:, cs].astype(F32), axis=0, keepdims=True)

    def patches(s, r, core):
        zs = lax.rem(z + s, NZ)
        yy = y if r == 0 else 1 - y
        return ph_ref.at[:, pl.ds(pl.multiple_of((zs * 4 + yy * 2 + core) * TB, TB), TB)]

    local, pre_in = {}, {}
    for s in ORDER:
        for r in range(2):
            local[s, r] = pltpu.make_async_copy(
                patches(s, r, c), pre.at[s, pl.ds(0, FB), pl.ds(r * TB, TB)], pre_l.at[s, r]
            )
            local[s, r].start()

    def pre_send(s):
        for r in range(2):
            pre_in[s, r] = send(
                patches(s, r, 1 - c), pre.at[s, pl.ds(FB, FB), pl.ds(r * TB, TB)],
                pre_s.at[s, r], pre_r.at[s, r], co,
            )

    w_in = {}

    def w_send(i):
        src, dst = ((wo_ref, wo), (wi_ref, wi))[i]
        w_in[i] = send(src, dst.at[pl.ds(FB, FB)], w_s.at[i], w_r.at[i], co)

    pre_send(0)
    col_s[pl.ds(0, FB)] = jnp.broadcast_to(si_ref[...], (128, FB)).T
    col_r[pl.ds(0, FB)] = jnp.broadcast_to(ro_ref[...], (128, FB)).T
    col_in = [
        send(b.at[pl.ds(0, FB)], b.at[pl.ds(FB, FB)], col_ss.at[i], col_sr.at[i], co)
        for i, b in enumerate((col_s, col_r))
    ]
    vec_out[0, pl.ds(7, 1)] = jnp.zeros((1, 128), F32)
    vec_out[0, pl.ds(15, 1)] = jnp.zeros((1, 128), F32)
    acc_ro[...] = jnp.zeros_like(acc_ro)
    acc_si[...] = jnp.zeros_like(acc_si)

    GT = 32

    def gelu(s, side):
        if side == 0:
            for r in range(2):
                local[s, r].wait()
        else:
            for r in range(2):
                pre_in[s, r].wait_recv()

        def tile(i, _):
            rows = pl.ds(pl.multiple_of(side * FB + i * GT, GT), GT)
            sc, rc = col_s[rows], col_r[rows]
            for j in range(2):
                cs = pl.ds(j * 128, 128)
                v = pre[s, rows, cs].astype(F32) * sc
                cdf = 0.5 * (1.0 + lax.erf(v * 0.7071067811865476))
                hid[s, rows, cs] = (v * cdf * rc).astype(BF)
                pdf = jnp.exp(-0.5 * v * v) * 0.3989422804014327
                slope[s, rows, cs] = (cdf + v * pdf) * rc
            return 0

        lax.fori_loop(0, FB // GT, tile, 0)

    UT = 240

    def grad_pre(s, side):
        need_slots(Z, (s,))

        def tile(i, _):
            rows = pl.ds(pl.multiple_of(side * FB + i * UT, 16), UT)
            u = lax.dot_general(wo[rows], z_all[s], (((1,), (1,)), ((), ())), preferred_element_type=F32)
            sc = col_s[rows]
            q = u * hid[s, rows].astype(F32)
            acc_ro[rows] += q[:, :128] + q[:, 128:]
            a = u * slope[s, rows]
            q = a * pre[s, rows].astype(F32)
            acc_si[rows] += q[:, :128] + q[:, 128:]
            gp[s, rows, pl.ds(0, 128)] = (a[:, :128] * sc).astype(BF)
            gp[s, rows, pl.ds(128, 128)] = (a[:, 128:] * sc).astype(BF)
            return 0

        lax.fori_loop(0, FB // UT, tile, 0)

    HT = 448

    def grad_h(s):
        def tile(i, _):
            rows = pl.ds(pl.multiple_of(i * HT, 16), HT)
            slope[s, rows] = jnp.dot(wt[rows], gp[s], preferred_element_type=F32)
            return 0

        lax.fori_loop(0, D // HT, tile, 0)

    WT = 240

    def grad_w(g, side, slots, first):
        lhs, rhs = (hid, z_all) if g == 0 else (gp, in_all)
        out, cols = (part if side else accs[g]), columns[g]
        need_slots(g, slots)

        def tile(i, _):
            rows = pl.ds(pl.multiple_of(i * WT, 16), WT)
            src = pl.ds(pl.multiple_of(side * FB + i * WT, 16), WT)
            for n, s in enumerate(slots):
                t = jnp.dot(lhs[s, src], rhs[s, :, cols], preferred_element_type=F32)
                if first and n == 0:
                    out[rows, cols] = t
                else:
                    out[rows, cols] += t
            return 0

        lax.fori_loop(0, FB // WT, tile, 0)

    accs = (gwo_ref, gwi_ref, gwi_ref)
    which = (0, 1, 1)
    stage = {}

    def piece(xx):
        return pl.ds(pl.multiple_of(112 * xx + 16 * (xx // 2), 16), 128)

    def w_sib(g):
        a, cols = which[g], columns[g]
        sib_out[a, :, cols] = part[:, cols].astype(BF)
        stage["sib", g] = send(sib_out.at[a, :, cols], sib_in.at[a, :, cols], sib_ss.at[g], sib_sr.at[g], co)

    def w_x(g):
        a, cols = which[g], columns[g]
        stage["sib", g].wait_recv()
        t = accs[g][:, cols] + sib_in[a, :, cols].astype(F32)
        accs[g][:, cols] = t
        mem_out[a, :, cols] = t.astype(BF)
        stage["x", g] = [
            send(
                mem_out.at[a, piece(lax.rem(x + k, 4)), cols], mem_x.at[a, k - 1, :, cols],
                x_s.at[g, k - 1], x_r.at[g, k - 1], xs[k - 1],
            )
            for k in (2, 1, 3)
        ]

    def w_h(g):
        a, cols = which[g], columns[g]
        for copy in stage["x", g]:
            copy.wait_recv()
        total = accs[g][piece(x), cols]
        for k in range(3):
            total += mem_x[a, k, :, cols].astype(F32)
        mem_h[a, 0, :, cols] = total.astype(BF)
        stage["h", g] = send(mem_h.at[a, 0, :, cols], mem_h.at[a, 1, :, cols], h_s.at[g], h_r.at[g], ho)

    def w_all(g):
        a, cols = which[g], columns[g]
        stage["h", g].wait_recv()
        mem_all[a, 0, :, cols] = (mem_h[a, 0, :, cols].astype(F32) + mem_h[a, 1, :, cols].astype(F32)).astype(BF)
        stage["all", g] = [
            send(mem_all.at[a, 0, :, cols], mem_all.at[a, k, :, cols], all_s.at[g, k - 1], all_r.at[g, k - 1], xs[k - 1])
            for k in (2, 1, 3)
        ]

    def w_end(g):
        a, cols = which[g], columns[g]
        for copy in stage["all", g]:
            copy.wait_recv()
        for xx in range(4):
            rows = pl.ds(112 * xx + 16 * (xx // 2), 128)
            gw_ref[a, rows, cols] = mem_all[a, lax.rem(x + 4 - xx, 4), :, cols]

    def v_part(g, side):
        grads = part if side else accs[g]
        for j in range(CA // 128) if g == 1 else range(CA // 128, D // 128):
            cs = pl.ds(j * 128, 128)
            t = jnp.sum(wi[pl.ds(side * FB, FB), cs].astype(F32) * grads[:, cs], axis=0, keepdims=True)
            if side == 1:
                vec_out[0, pl.ds(8 + j, 1)] = t
            else:
                vec_out[0, pl.ds(8 + j, 1)] += t

    def v_pair(i, dev):
        stage["v", i] = send(vec_out.at[i], vec_in.at[i], vec_ss.at[i], vec_sr.at[i], dev)

    def v_sum(i):
        stage["v", i].wait_recv()
        t = vec_out[i] + vec_in[i]
        if i == 0:
            vec_out[1] = t
        else:
            vec_z[0] = t

    def v_send():
        stage["vz"] = [
            send(vec_z.at[0], vec_z.at[NZ - k], vz_s.at[k - 1], vz_r.at[k - 1], zs_all[k - 1]) for k in range(1, NZ)
        ]

    def v_end():
        for copy in stage["vz"]:
            copy.wait_recv()
        total = vec_z[lax.rem(NZ - z, NZ)]
        for s in range(1, NZ):
            total += vec_z[lax.rem(s + NZ - z, NZ)]
        for j in range(D // 128):
            cs = pl.ds(j * 128, 128)
            gso_ref[:, cs] = total[j:j + 1] * (1.0 / 64.0)
            gri_ref[:, cs] = total[8 + j:9 + j] / ri_ref[:, cs] * (1.0 / 64.0)

    def acc_send():
        stage["acc"] = [
            send(b.at[pl.ds(FB, FB)], acc_in.at[i], acc_ss.at[i], acc_sr.at[i], co)
            for i, b in enumerate((acc_ro, acc_si))
        ]

    def acc_end():
        for copy in stage["acc"]:
            copy.wait_recv()
        t = (acc_ro[pl.ds(0, FB)] + acc_in[0]) / col_r[pl.ds(0, FB)]
        gro_ref[...] = jnp.sum(t.T, axis=0, keepdims=True) * (1.0 / 64.0)
        t = acc_si[pl.ds(0, FB)] + acc_in[1]
        gsi_ref[...] = jnp.sum(t.T, axis=0, keepdims=True) * (1.0 / 64.0)

    def transpose_w():
        w_in[1].wait_recv()
        w_copies[1].wait()
        for j in range(D // 128):
            cs = pl.ds(j * 128, 128)
            wt[cs, :] = wi[:, cs].astype(F32).T.astype(BF)

    def wait_wo():
        w_in[0].wait_recv()
        w_copies[0].wait()

    def sum_send(step, p):
        rows = pl.ds(*SUM_ROWS[p])
        hops = [*HOPS[:14], LAST[p]]
        if p == 0:
            hops[5] = (0, (0, 1), (7, 1))
        if p == 1:
            hops[8] = (1, (0, 1), (1, 1))
        for k in SUM_STEPS[step]:
            way, _, (ds, dr) = hops[k]
            t = slope[ds, rows, pl.ds(dr * TB, TB)]
            for k2 in range(15):
                if hops[k2][1] == (ds, dr):
                    need(R, k2, p)
                    t += rbuf[k2, rows].astype(F32)
            sbuf[k, rows] = t.astype(BF)
            send(sbuf.at[k, rows], rbuf.at[k, rows], ring_s.at[R, k, p], ring_r.at[R, k, p], (zm, zp, yo)[way])

    def col_wait():
        for copy in col_in:
            copy.wait_recv()

    f = functools.partial
    early, late = ORDER[:5], ORDER[5:]
    plan = (
        (Z, 0, 0, f(pre_send, 7), f(gelu, 0, 0)),
        (Z, 0, 1, f(w_send, 0), f(gelu, 7, 0)),
        (Z, 0, 2, f(pre_send, 1), f(gelu, 1, 0)),
        (Z, 0, 3, f(pre_send, 2), f(gelu, 2, 0)),
        (Z, 1, 0, f(pre_send, 6), col_wait, f(gelu, 0, 1)),
        (Z, 1, 1, f(w_send, 1), f(gelu, 7, 1)),
        (Z, 1, 2, f(pre_send, 5), f(gelu, 1, 1)),
        (Z, 1, 3, wait_wo, f(grad_pre, 0, 0)),
        (Z, 2, 0, f(pre_send, 3), f(grad_pre, 0, 1)),
        (Z, 2, 1, f(pre_send, 4), f(gelu, 6, 0), f(gelu, 6, 1)),
        (Z, 2, 2, f(gelu, 2, 1), f(gelu, 5, 0)),
        (Z, 2, 3, f(grad_pre, 7, 0)),
        (A, 0, 0, f(grad_pre, 7, 1)),
        (A, 0, 1, f(gelu, 5, 1), f(gelu, 3, 0)),
        (Z, 3, 0, f(gelu, 3, 1)),
        (Z, 3, 1, f(gelu, 4, 0)),
        (Z, 3, 2, f(gelu, 4, 1)),
        (Z, 3, 3, f(grad_pre, 1, 0)),
        (Z, 4, 0, f(grad_pre, 1, 1)),
        (Z, 4, 1, f(grad_w, 0, 1, ORDER[:3], True)),
        (Z, 4, 2, f(grad_w, 0, 0, ORDER[:3], True)),
        (Z, 4, 3, f(grad_pre, 2, 0)),
        (A, 1, 0, transpose_w, f(grad_pre, 2, 1)),
        (A, 1, 1, f(grad_w, 0, 1, (2, 6), False)),
        (B, 0, 0, f(grad_w, 0, 1, late, False), f(w_sib, 0)),
        (B, 0, 1, f(grad_w, 0, 0, (2, 6, *late), False)),
        (A, 2, 0, f(grad_pre, 6, 0)),
        (A, 2, 1, f(w_x, 0), f(grad_pre, 6, 1)),
        (B, 1, 0, f(grad_pre, 5, 0)),
        (B, 1, 1, f(grad_pre, 5, 1)),
        (A, 3, 0, f(grad_pre, 3, 0)),
        (A, 3, 1, f(grad_pre, 3, 1)),
        (B, 2, 0, f(grad_pre, 4, 0)),
        (B, 2, 1, f(grad_pre, 4, 1), acc_send),
        (A, 4, 0, f(grad_h, 4), f(grad_h, 7)),
        (A, 4, 1, f(grad_h, 5), f(grad_h, 3)),
        (B, 3, 0, f(grad_w, 1, 1, early, True)),
        (B, 3, 1, f(w_h, 0), f(grad_w, 1, 0, early, True)),
        (R, 5, 0, f(grad_h, 2)),
        (R, 5, 1, f(grad_w, 1, 1, late, False), f(w_sib, 1)),
        (R, 5, 2, f(grad_w, 1, 0, late, False), f(v_part, 1, 1)),
        (R, 5, 3, f(v_part, 1, 0), f(grad_h, 6)),
        (R, 4, 0, f(w_x, 1)),
        (R, 4, 1, f(grad_h, 1)),
        (B, 4, 0),
        (B, 4, 1, f(grad_w, 2, 1, early, True)),
        (R, 4, 2, f(w_all, 0), f(grad_w, 2, 0, early, True)),
        (R, 4, 3, f(grad_h, 0)),
        (R, 3, 0, f(grad_w, 2, 1, late, False), f(w_sib, 2)),
        (R, 3, 1, f(grad_w, 2, 0, late, False), f(v_part, 2, 1), f(v_part, 2, 0)),
        (R, 3, 2, f(w_x, 2), f(v_pair, 0, co)),
        (R, 3, 3, f(w_h, 1)),
        (R, 2, 0, f(v_sum, 0), f(v_pair, 1, yo)),
        (R, 2, 1, acc_end),
        (R, 2, 2),
        (R, 2, 3, f(w_all, 1)),
        (R, 1, 0, f(v_sum, 1), v_send),
        (R, 1, 1),
        (R, 1, 2, f(w_h, 2)),
        (R, 1, 3),
        (R, 0, 0),
        (R, 0, 1, f(w_end, 0)),
        (R, 0, 2),
        (R, 0, 3, f(w_all, 2), v_end, f(w_end, 1)),
    )
    marks = [len(sent)]
    for n, (u, step, p, *work) in enumerate(plan):
        if u == R:
            sum_send(step, p)
        elif n >= PARTS[Z]:
            gather_send(u, step, p)
        for job in work:
            job()
        marks.append(len(sent))
        if n >= 16:
            for copy in sent[marks[n - 16]:marks[n - 15]]:
                copy.wait_send()
    for p in range(PARTS[R]):
        for k in range(3):
            need(R, k, p)
        at, size = SUM_ROWS[p]
        for j in range(at, at + size, 128):
            cs = pl.ds(j, 128)
            t = slope[0, cs, pl.ds(0, TB)]
            for k in range(3):
                t += rbuf[k, cs].astype(F32)
            gx_ref[:, cs] = t.T * ri_ref[:, cs]
    for copy in (*sent[:marks[0]], *sent[marks[len(plan) - 16]:]):
        copy.wait_send()
    w_end(2)


def finish(gx, gw, gri, gsi, gro, gso, gx_out, gwi_out, gwo_out, gri_out, gsi_out, gro_out, gso_out):
    gwo_out[...] = gw[0].astype(F32) * WSCALE
    gwi_out[...] = gw[1].astype(F32) * WSCALE
    gx_out[...] = gx[...]

    @pl.when(pl.program_id(0) == 0)
    def _():
        for src, dst in ((gri, gri_out), (gsi, gsi_out), (gro, gro_out), (gso, gso_out)):
            dst[...] = src[...]


def per_device(
    inputs, cotangent, counts, pre_hidden, pre_out, w_in, w_out, r_in, s_in, r_out, s_out
):
    vm, hbm = pl.BlockSpec(memory_space=pltpu.VMEM), pl.BlockSpec(memory_space=pl.ANY)
    dma = pltpu.SemaphoreType.DMA
    shapes = (((TB, D), F32), ((2, FB, D), BF), ((1, D), F32), ((1, FB), F32), ((1, FB), F32), ((1, D), F32))
    outs = pl.pallas_call(
        kernel,
        out_shape=[jax.ShapeDtypeStruct(shape, dtype) for shape, dtype in shapes],
        in_specs=[hbm, hbm, vm, hbm, hbm, hbm, hbm, vm, vm, vm, vm],
        out_specs=[vm] * 6,
        scratch_shapes=[
            *[pltpu.VMEM((TB, D), BF)] * 3,
            dma((3,)),
            pltpu.VMEM((FB, D), F32),
            pltpu.VMEM((FB, D), F32),
            pltpu.VMEM((NZ, NF, 2 * TB), BF),
            pltpu.VMEM((NZ, NF, 2 * TB), F32),
            pltpu.VMEM((NZ, NF, 2 * TB), BF),
            pltpu.VMEM((NZ, NF, 2 * TB), BF),
            pltpu.VMEM((NZ, 2 * TB, D), BF),
            pltpu.VMEM((NZ, 2 * TB, D), BF),
            pltpu.VMEM((NF, D), BF),
            pltpu.VMEM((NF, D), BF),
            pltpu.VMEM((D, NF), BF),
            pltpu.VMEM((15, D, TB), BF),
            pltpu.VMEM((15, D, TB), BF),
            pltpu.VMEM((NF, 128), F32),
            pltpu.VMEM((NF, 128), F32),
            pltpu.VMEM((2, FB, 128), F32),
            pltpu.VMEM((NF, 128), F32),
            pltpu.VMEM((NF, 128), F32),
            pltpu.VMEM((FB, D), F32),
            pltpu.VMEM((2, FB, D), BF),
            pltpu.VMEM((2, FB, D), BF),
            pltpu.VMEM((2, FB, D), BF),
            pltpu.VMEM((2, 3, 128, D), BF),
            pltpu.VMEM((2, 2, 128, D), BF),
            pltpu.VMEM((2, 4, 128, D), BF),
            pltpu.VMEM((2, 16, 128), F32),
            pltpu.VMEM((2, 16, 128), F32),
            pltpu.VMEM((NZ, 16, 128), F32),
            dma((4, 15, 4)), dma((4, 15, 4)),
            dma((NZ, 2)), dma((NZ, 2)), dma((NZ, 2)),
            dma((2,)), dma((2,)), dma((2,)),
            dma((2,)), dma((2,)),
            dma((2,)), dma((2,)),
            dma((3,)), dma((3,)),
            dma((3, 3)), dma((3, 3)),
            dma((3,)), dma((3,)),
            dma((3, 3)), dma((3, 3)),
            dma((2,)), dma((2,)),
            dma((7,)), dma((7,)),
        ],
        compiler_params=pltpu.CompilerParams(
            collective_id=0, has_side_effects=True, vmem_limit_bytes=63 * 2**20
        ),
    )(inputs[0], cotangent[0], counts, pre_hidden[0], pre_out[0], w_in, w_out, r_in, s_in, r_out, s_out)
    steps = 3
    rows = pl.BlockSpec((FB // steps, D), lambda i: (i, 0))
    some = pl.BlockSpec((TB // 2, D), lambda i: (jnp.minimum(i, 1), 0))
    small = [pl.BlockSpec(shape, lambda i: (0, 0)) for shape, _ in shapes[2:]]
    gx, gwi, gwo, gri, gsi, gro, gso = pl.pallas_call(
        finish,
        grid=(steps,),
        out_shape=[
            jax.ShapeDtypeStruct(shape, F32)
            for shape in ((TB, D), (FB, D), (FB, D), (1, D), (1, FB), (1, FB), (1, D))
        ],
        in_specs=[some, pl.BlockSpec((2, FB // steps, D), lambda i: (0, i, 0)), *small],
        out_specs=[some, rows, rows, *small],
        compiler_params=pltpu.CompilerParams(vmem_limit_bytes=63 * 2**20),
    )(*outs)
    return gx[None], gwi, gwo, gri, gsi, gro, gso


def solution(mesh):
    return jax.shard_map(
        per_device,
        mesh=mesh,
        in_specs=(
            P("member", "dp", None),
            P("member", "dp", None),
            P("member", "dp"),
            P("member", "dp", None),
            P("member", "dp", None),
            P("dp", None),
            P("dp", None),
            P("member", None),
            P("member", "dp"),
            P("member", "dp"),
            P("member", None),
        ),
        out_specs=(
            P("member", "dp", None),
            P("dp", None),
            P("dp", None),
            P("member", None),
            P("member", "dp"),
            P("member", "dp"),
            P("member", None),
        ),
        check_vma=False,
    )
```
